128 devices in a mesh: chan: 16 (over x, z), blk: 8 (over y, core).
Axes of the slice: x: 4, y: 4, z: 4, core: 2. Of those that a mesh axis runs over, the one named last changes fastest.
Arguments:
- pp_amps: bfloat16 [32, 3072, 3072], P('chan', 'blk'), may hold values from -6 to 6
- ph_coupling: bfloat16 [32, 3072, 3072], P('chan'), may hold values from -0.109375 to 0.109375
- pp_coupling: bfloat16 [32, 3072, 3072], P('chan', 'blk'), may hold values from -6 to 6
- sixj: float32 [2, 32, 384], replicated, may hold values from -1.5 to 1.5
- src_map: int32 [2, 32, 384], replicated, may hold values from 0 to 12287, as said below
- live_rows: int32 [32], replicated, may hold values from 1 to 3072, 49152 in all
Outputs:
- cycle_pp: bfloat16 [32, 3072, 3072], P('chan', 'blk')
- energy: float32 [], replicated
The draws below stay inside these ranges and needn't reach their ends.
Inputs may be any that keep to these rules, and one draw needn't show every extreme that they name: For each term s, src_map[s] names every particle-particle tile exactly once. The two sources of a particle-hole tile lie in the same particle-particle channel, and in the same row block as the particle-hole tile (the rows held by one index of blk). Within one row block, the particle-hole tiles of the channels of any one chan index take their sources from every chan index equally often. `live_rows`: the largest is exactly 3072.
All inputs are finite; a program needn't handle non-finite values.
Results may differ from the reference program's by a relative error of at most 0.04.
Values may be sent and summed in bfloat16 or wider, within the bound.
No kernel may reach another device: no remote copies, remote signals or barrier semaphores. Data moves between devices by JAX's collectives and lax.ppermute only.
A program may use at most 256 MiB of HBM per device.

```python
import math
import jax
import jax.numpy as jnp
import numpy as np
from jax import lax

NPH = 3072
TILE = 8
CH_DEV = 2
NCH = 32
NT = 384
N_CHAN = 16
N_BLK = 8


def draw_src_map(key, part):
    key = jax.random.fold_in(key, 11)
    tiles_dev = NT // N_BLK
    slot_count = CH_DEV * tiles_dev
    bucket = slot_count // N_CHAN

    def permuted(subkey):
        return jax.random.permutation(subkey, slot_count)
    split_keys = jax.random.split(key, 3)
    dest_order = jax.vmap(permuted)(jax.random.split(split_keys[0], N_BLK * N_CHAN)).reshape(N_BLK, N_CHAN, slot_count)
    source_order = jax.vmap(permuted)(jax.random.split(split_keys[1], N_BLK * N_CHAN)).reshape(N_BLK, N_CHAN, slot_count)
    shifts = jax.random.randint(split_keys[2], (N_BLK, N_CHAN, CH_DEV), 1, tiles_dev)
    blk_ids = jnp.arange(N_BLK, dtype=jnp.int32)[:, None, None]
    dest_ids = jnp.arange(N_CHAN, dtype=jnp.int32)[None, :, None]
    source_dev = (dest_ids + dest_order // bucket) % N_CHAN
    first_slot = source_order[blk_ids, source_dev, dest_order]
    chan_local = first_slot // tiles_dev
    first_tile = first_slot % tiles_dev
    second_tile = (first_tile + shifts[blk_ids, source_dev, chan_local]) % tiles_dev
    channel = source_dev * CH_DEV + chan_local
    base_index = channel * NT + blk_ids * tiles_dev
    stacked = jnp.stack([base_index + first_tile, base_index + second_tile])
    stacked = stacked.reshape(2, N_BLK, N_CHAN, CH_DEV, tiles_dev).transpose(0, 2, 3, 1, 4)
    return stacked.reshape(2, NCH, NT).astype(jnp.int32)


def steps_of(key, dims, shards, least, top_value):
    factor_of = 1.0
    for dim, parts in shards:
        heights = jax.random.uniform(jax.random.fold_in(jax.random.fold_in(key, 6), dim), (parts,), jnp.float32, least / len(shards), top_value / len(shards))
        factor_of = factor_of * jnp.repeat(jnp.exp(heights), dims[dim] // parts).reshape((-1,) + (1,) * (len(dims) - 1 - dim))
    return factor_of


def length_profile(count, total, bound, skew):
    loads = [(1 << 20) // math.isqrt(standing ** skew) + 1 for standing in range(2, count + 1)]
    surplus, given = total - bound - (count - 1), [1] * (count - 1)
    while surplus > 0:
        movable = [i for i in range(count - 1) if given[i] < bound]
        pool, budget = sum([loads[i] for i in movable]), surplus
        for i in movable:
            addition = min(bound - given[i], max(1, budget * loads[i] // pool), surplus)
            given[i] = given[i] + addition
            surplus = surplus - addition
    return np.array([bound] + given)


def uneven_parts(stream_key, count, total, most, slope):
    if count == 2:
        one = jax.random.randint(stream_key, (), max(1, total - most), min(most, total - 1) + 1)
        return jnp.stack([one, total - one])
    tallies = jnp.asarray(length_profile(count, total, most, slope), jnp.int32)
    pairs = (count - 1) // 2
    giver, sink = tallies[1:1 + 2 * pairs:2], tallies[2:2 + 2 * pairs:2]
    room = jnp.minimum(giver - 1, most - sink)
    passed = jax.random.randint(jax.random.fold_in(stream_key, 1), (pairs,), 0, 1 << 20) % (room + 1)
    tallies = tallies.at[1:1 + 2 * pairs:2].set(giver - passed).at[2:2 + 2 * pairs:2].set(sink + passed)
    return tallies[jax.random.permutation(jax.random.fold_in(stream_key, 2), count)]


def centred(stream_key, shape, spread, most, pieces=(), kind=jnp.bfloat16):
    entries = jax.random.normal(stream_key, shape, jnp.float32) * spread
    if len(pieces) > 0:
        entries = steps_of(stream_key, shape, pieces, -0.22, 0.18) * entries
    return jnp.clip(entries, min=-most, max=most).astype(kind)


def setup_inputs(seed: int = 0) -> dict:
    seeds = jax.random.split(jax.random.key(seed), 7)
    pp_amps = centred(seeds[0], (NCH, NPH, NPH), 1.0, 6.0, ((0, 16), (1, 8)))
    ph_coupling = centred(seeds[1], (NCH, NPH, NPH), NPH ** -0.5, 0.109375, ((0, 16),))
    pp_coupling = centred(seeds[2], (NCH, NPH, NPH), 1.0, 6.0, ((0, 16), (1, 8)))
    sixj = jnp.clip(jax.random.uniform(seeds[3], (2, NCH, NT), jnp.float32, -1.5, 1.5), -1.5, 1.5)
    src_map = draw_src_map(jax.random.fold_in(seeds[6], 71), 0)
    live_rows = uneven_parts(seeds[5], NCH, NCH * NPH // 2, NPH, 2).astype(jnp.int32)
    return dict(pp_amps=pp_amps, ph_coupling=ph_coupling, pp_coupling=pp_coupling, sixj=sixj, src_map=src_map, live_rows=live_rows)


def channel_product(pair):
    return jnp.dot(pair[0], pair[1], preferred_element_type=jnp.float32).astype(jnp.bfloat16)

def reference(pp_amps, ph_coupling, pp_coupling, sixj, src_map, live_rows):
    pp_tiles = pp_amps.reshape(NCH * NT, TILE, NPH)
    row_index = jnp.arange(NT, dtype=jnp.int32)[:, None] * TILE + jnp.arange(TILE, dtype=jnp.int32)[None, :]
    live_mask = row_index[None, :, :] < live_rows[:, None, None]
    first_map = src_map[0].reshape(-1)
    second_map = src_map[1].reshape(-1)
    first_coef = sixj[0].reshape(-1)[:, None, None]
    second_coef = sixj[1].reshape(-1)[:, None, None]
    first_term = pp_tiles[first_map].astype(jnp.float32)
    second_term = pp_tiles[second_map].astype(jnp.float32)
    recoupled = first_coef * first_term + second_coef * second_term
    recoupled = jnp.where(live_mask.reshape(NCH * NT, TILE)[:, :, None], recoupled, 0.0)
    ph_amps = recoupled.astype(jnp.bfloat16).reshape(NCH, NPH, NPH)
    cycle_rows = lax.map(channel_product, (ph_amps, ph_coupling))
    cycle_tiles = cycle_rows.reshape(NCH * NT, TILE, NPH).astype(jnp.float32)
    summed = jnp.zeros((NCH * NT, TILE, NPH), jnp.float32)
    summed = summed.at[first_map].add(first_coef * cycle_tiles)
    summed = summed.at[second_map].add(second_coef * cycle_tiles)
    cycle_pp = summed.astype(jnp.bfloat16).reshape(NCH, NPH, NPH)
    energy = jnp.sum(cycle_pp.astype(jnp.float32) * pp_coupling.astype(jnp.float32)) / (NPH * math.sqrt(NCH))
    return (cycle_pp, energy)
```

```python
import math

import jax
import jax.numpy as jnp
from jax import lax
from jax.experimental import pallas as pl
from jax.experimental.pallas import tpu as pltpu
from jax.sharding import PartitionSpec as P

TILE = 8
VMEM_BYTES = 56 * 1024 * 1024


def combine_kernel(index_ref, coef_ref, tiles_ref, send_ref):
    columns = tiles_ref.shape[2]
    row = lax.broadcasted_iota(jnp.int32, (TILE, columns), 0)

    def one(slot, carry):
        first = tiles_ref[index_ref[0, slot]].astype(jnp.float32)
        second = tiles_ref[index_ref[1, slot]].astype(jnp.float32)
        value = coef_ref[0, slot] * first + coef_ref[1, slot] * second
        value = jnp.where(row < index_ref[2, slot], value, 0.0)
        send_ref[slot] = value.astype(jnp.bfloat16)
        return carry

    lax.fori_loop(0, send_ref.shape[0], one, 0, unroll=4)


def combine(index, coef, tiles, block):
    slots, _, columns = tiles.shape
    spec = pl.BlockSpec((slots, TILE, block), lambda n, *_: (0, 0, n))
    return pl.pallas_call(
        combine_kernel,
        grid_spec=pltpu.PrefetchScalarGridSpec(
            num_scalar_prefetch=2,
            grid=(columns // block,),
            in_specs=[spec],
            out_specs=spec,
        ),
        out_shape=jax.ShapeDtypeStruct(tiles.shape, jnp.bfloat16),
        compiler_params=pltpu.CompilerParams(vmem_limit_bytes=VMEM_BYTES),
        cost_estimate=pl.CostEstimate(
            flops=4 * tiles.size, bytes_accessed=4 * tiles.size, transcendentals=0
        ),
    )(index, coef, tiles)


def product_kernel(arrival_ref, x_ref, w_ref, out_ref, ordered):
    n, c = pl.program_id(0), pl.program_id(1)
    slots = x_ref.shape[0]
    half = slots // 2

    @pl.when((n == 0) & (c == 0))
    def _():
        def one(j, carry):
            ordered[j] = x_ref[arrival_ref[j]]
            return carry

        lax.fori_loop(0, slots, one, 0, unroll=4)

    rows = ordered[pl.ds(c * half, half)].reshape(half * TILE, x_ref.shape[2])
    result = jnp.dot(rows, w_ref[0], preferred_element_type=jnp.float32)
    result = result.astype(jnp.bfloat16).reshape(half, TILE, result.shape[1])
    for i in range(half):
        out_ref[arrival_ref[c * half + i]] = result[i]


def product(arrival, x, w, block):
    slots, _, columns = x.shape
    return pl.pallas_call(
        product_kernel,
        grid_spec=pltpu.PrefetchScalarGridSpec(
            num_scalar_prefetch=1,
            grid=(columns // block, 2),
            in_specs=[
                pl.BlockSpec((slots, TILE, columns), lambda n, c, *_: (0, 0, 0)),
                pl.BlockSpec((1, columns, block), lambda n, c, *_: (c, 0, n)),
            ],
            out_specs=pl.BlockSpec((slots, TILE, block), lambda n, c, *_: (0, 0, n)),
            scratch_shapes=[pltpu.VMEM((slots, TILE, columns), jnp.bfloat16)],
        ),
        out_shape=jax.ShapeDtypeStruct(x.shape, jnp.bfloat16),
        compiler_params=pltpu.CompilerParams(vmem_limit_bytes=VMEM_BYTES),
        cost_estimate=pl.CostEstimate(
            flops=2 * x.size * columns,
            bytes_accessed=4 * x.size + 2 * w.size,
            transcendentals=0,
        ),
    )(arrival, x, w)


def finish_kernel(index_ref, coef_ref, back_ref, pair_ref, out_ref, energy_ref, total):
    n = pl.program_id(0)

    @pl.when(n == 0)
    def _():
        total[...] = jnp.zeros_like(total)

    def one(g, acc):
        at0, at1 = index_ref[0, g], index_ref[1, g]
        value = coef_ref[0, at0] * back_ref[at0].astype(jnp.float32)
        value = value + coef_ref[1, at1] * back_ref[at1].astype(jnp.float32)
        out_ref[g] = value.astype(jnp.bfloat16)
        return acc + value * pair_ref[g].astype(jnp.float32)

    total[...] += lax.fori_loop(
        0, out_ref.shape[0], one, jnp.zeros(total.shape, jnp.float32), unroll=4
    )

    @pl.when(n == pl.num_programs(0) - 1)
    def _():
        sums = jnp.sum(total[...], axis=0, keepdims=True)
        energy_ref[...] = jnp.broadcast_to(jnp.sum(sums), energy_ref.shape)


def finish(index, coef, back, pair, block, copies):
    slots, _, columns = back.shape
    spec = pl.BlockSpec((slots, TILE, block), lambda n, *_: (0, 0, n))
    return pl.pallas_call(
        finish_kernel,
        grid_spec=pltpu.PrefetchScalarGridSpec(
            num_scalar_prefetch=2,
            grid=(columns // block,),
            in_specs=[spec, spec],
            out_specs=[spec, pl.BlockSpec((copies, 128), lambda n, *_: (0, 0))],
            scratch_shapes=[pltpu.VMEM((TILE, block), jnp.float32)],
        ),
        out_shape=[
            jax.ShapeDtypeStruct(back.shape, jnp.bfloat16),
            jax.ShapeDtypeStruct((copies, 128), jnp.float32),
        ],
        compiler_params=pltpu.CompilerParams(vmem_limit_bytes=VMEM_BYTES),
        cost_estimate=pl.CostEstimate(
            flops=6 * back.size, bytes_accessed=6 * back.size, transcendentals=0
        ),
    )(index, coef, back, pair)


def on_device(pp_amps, ph_coupling, pp_coupling, sixj, src_map, live_rows):
    chan_count = lax.axis_size("chan")
    blk_count = lax.axis_size("blk")
    chan_index = lax.axis_index("chan")
    blk_index = lax.axis_index("blk")
    chans_dev, rows_dev, columns = pp_amps.shape
    tiles_dev = rows_dev // TILE
    slots = chans_dev * tiles_dev
    bucket = slots // chan_count
    all_tiles = src_map.shape[2]

    def slab(array):
        part = lax.dynamic_slice_in_dim(array, blk_index * tiles_dev, tiles_dev, 2)
        return part.reshape(2, chan_count, slots)

    slab_map, slab_coef = slab(src_map), slab(sixj)
    channel = slab_map // all_tiles
    source_dev = channel[0] // chans_dev
    local_slot = channel % chans_dev * tiles_dev + slab_map % all_tiles % tiles_dev
    first_row = (blk_index * tiles_dev + jnp.arange(tiles_dev, dtype=jnp.int32)) * TILE
    live = jnp.clip(live_rows[:, None] - first_row[None, :], 0, TILE).reshape(chan_count, slots)
    ids = jnp.arange(slots, dtype=jnp.int32)

    mine = source_dev == chan_index
    before = ids[None, :] <= ids[:, None]
    rank = jnp.sum((mine[:, None, :] & before[None]).astype(jnp.int32), axis=2) - 1
    wanted = mine[:, None, :] & (
        rank[:, None, :] == jnp.arange(bucket, dtype=jnp.int32)[None, :, None]
    )

    def pick(values):
        return jnp.sum(jnp.where(wanted, values[:, None, :], 0), axis=2).reshape(slots)

    send_index = jnp.stack([pick(local_slot[0]), pick(local_slot[1]), pick(live)])
    send_coef = jnp.stack([pick(slab_coef[0]), pick(slab_coef[1])])

    source_mine = jnp.take(source_dev, chan_index, axis=0)
    earlier = (source_mine[None, :] == source_mine[:, None]) & (ids[None, :] < ids[:, None])
    arrival = source_mine * bucket + jnp.sum(earlier.astype(jnp.int32), axis=1)

    took = jnp.sum(
        jnp.where(send_index[:2, None, :] == ids[None, :, None], ids[None, None, :], 0), axis=2
    )

    send_index, send_coef, arrival, took = lax.optimization_barrier(
        (send_index, send_coef, arrival, took)
    )
    own_tiles = pp_amps.reshape(slots, TILE, columns)
    sent = combine(send_index, send_coef, own_tiles, 512)
    got = lax.all_to_all(
        sent.reshape(chan_count, bucket, TILE, columns), "chan", 0, 0, tiled=True
    ).reshape(slots, TILE, columns)
    cycle_tiles = product(arrival, got, ph_coupling, 1024)
    back = lax.all_to_all(
        cycle_tiles.reshape(chan_count, bucket, TILE, columns), "chan", 0, 0, tiled=True
    ).reshape(slots, TILE, columns)
    cycle_pp, partial = finish(
        took, send_coef, back, pp_coupling.reshape(slots, TILE, columns), 512, chan_count * blk_count
    )
    parts = lax.all_to_all(partial, ("chan", "blk"), 0, 0, tiled=True)
    energy = jnp.sum(parts[:, 0]) / (columns * math.sqrt(chan_count * chans_dev))
    return (cycle_pp.reshape(pp_amps.shape), energy)


def solution(mesh):
    in_specs = (
        P("chan", "blk", None),
        P("chan", None, None),
        P("chan", "blk", None),
        P(),
        P(),
        P(),
    )
    out_specs = (P("chan", "blk", None), P())
    return jax.shard_map(
        on_device, mesh=mesh, in_specs=in_specs, out_specs=out_specs, check_vma=False
    )
```

```python
import functools
import math

import jax
import jax.numpy as jnp
from jax import lax
from jax.experimental import pallas as pl
from jax.experimental.pallas import tpu as pltpu
from jax.sharding import PartitionSpec as P

TILE = 8
LANES = 128
INTS = 3
COEFS = 2


def params(mib):
    return pltpu.CompilerParams(vmem_limit_bytes=mib * 1024 * 1024)


def any_spec():
    return pl.BlockSpec(memory_space=pl.ANY)


def column_copies(source, target, sems, count):
    width = source.shape[2] // count
    return [
        pltpu.make_async_copy(
            source.at[:, :, pl.ds(i * width, width)], target.at[:, :, pl.ds(i * width, width)], sems.at[i]
        )
        for i in range(count)
    ]


def floor_div(values, number):
    return jnp.floor((values.astype(jnp.float32) + 0.5) * (1.0 / number)).astype(jnp.int32)


def recouple_kernel(
    sizes, live_ref, map_hbm, sixj_hbm, tiles_ref, send_ref, ints_ref, coefs_ref, arrival_ref,
    held, made, map_ref, sixj_ref, map_buffer, sixj_buffer, ints, coefs, in_sem, out_sem, table_sem,
):
    chan_count, chans_dev, tiles_dev, all_tiles, chunks = sizes
    slots = chans_dev * tiles_dev
    bucket = slots // chan_count
    incoming = column_copies(tiles_ref, held, in_sem, chunks)
    outgoing = column_copies(made, send_ref, out_sem, chunks)
    from_hbm = [
        pltpu.make_async_copy(map_hbm, map_ref, table_sem.at[2]),
        pltpu.make_async_copy(sixj_hbm, sixj_ref, table_sem.at[3]),
    ]
    for copy in from_hbm + incoming:
        copy.start()

    me = lax.axis_index("chan")
    blk = lax.axis_index("blk")
    lane = lax.broadcasted_iota(jnp.int32, (chan_count, LANES), 1)

    def slab(ref, buffer, term):
        whole = None
        for c in range(chans_dev):
            shift = lax.rem((c - blk) * tiles_dev + all_tiles, all_tiles)
            buffer[term, c] = pltpu.roll(ref[term], shift, axis=1)[:, :LANES]
            rows = buffer[term, c, pl.ds(c, chan_count, stride=chans_dev), :]
            whole = rows if c == 0 else jnp.where(lane < c * tiles_dev, whole, rows)
        return whole

    for copy in from_hbm:
        copy.wait()
    source = None
    local = []
    for term in range(2):
        entry = slab(map_ref, map_buffer, term)
        channel = floor_div(entry, all_tiles)
        owner = floor_div(channel, chans_dev)
        tile = entry - channel * all_tiles - blk * tiles_dev
        local.append((channel - owner * chans_dev) * tiles_dev + tile)
        source = owner if source is None else source
    weight = [slab(sixj_ref, sixj_buffer, term) for term in range(2)]

    mine = (lane < slots) & (source == me)
    at = lax.broadcasted_iota(jnp.int32, (LANES, LANES), 0)
    to = lax.broadcasted_iota(jnp.int32, (LANES, LANES), 1)
    upto = (at <= to).astype(jnp.bfloat16)
    rank = jnp.dot(mine.astype(jnp.bfloat16), upto, preferred_element_type=jnp.float32)
    rank = rank.astype(jnp.int32) - 1
    int_table = jnp.zeros((chan_count, LANES), jnp.int32)
    coef_table = jnp.zeros((chan_count, LANES), jnp.float32)
    for r in range(bucket):
        chosen = mine & (rank == r)
        for f, values in enumerate((local[0], local[1], lane)):
            value = jnp.sum(jnp.where(chosen, values, 0), axis=1, keepdims=True)
            int_table = jnp.where(lane == r * INTS + f, value, int_table)
        for f, values in enumerate(weight):
            value = jnp.sum(jnp.where(chosen, values, 0.0), axis=1, keepdims=True)
            coef_table = jnp.where(lane == r * COEFS + f, value, coef_table)
    ints_ref[...] = int_table
    coefs_ref[...] = coef_table
    to_smem = [
        pltpu.make_async_copy(ints_ref, ints, table_sem.at[0]),
        pltpu.make_async_copy(coefs_ref, coefs, table_sem.at[1]),
    ]
    for copy in to_smem:
        copy.start()

    row = lax.broadcasted_iota(jnp.int32, (chan_count, LANES), 0)
    own = jnp.sum(jnp.where(row == me, source, 0), axis=0, keepdims=True)
    across = jnp.broadcast_to(own, (LANES, LANES))
    earlier = (across.T == across) & (at < to)
    arrival = own * bucket + jnp.sum(earlier.astype(jnp.int32), axis=0, keepdims=True)
    arrival_ref[...] = jnp.broadcast_to(arrival, arrival_ref.shape)

    for copy in to_smem:
        copy.wait()
    width = held.shape[2] // chunks
    tile_row = lax.broadcasted_iota(jnp.int32, (TILE, width), 0)
    for i in range(chunks):
        incoming[i].wait()
        columns = pl.ds(i * width, width)

        def to_one(d, carry):
            for r in range(bucket):
                slot = ints[d, r * INTS + 2]
                c = slot // tiles_dev
                first_row = (blk * tiles_dev + slot - c * tiles_dev) * TILE
                live = live_ref[d * chans_dev + c] - first_row
                value = coefs[d, r * COEFS] * held[ints[d, r * INTS], :, columns].astype(jnp.float32)
                value = value + coefs[d, r * COEFS + 1] * held[
                    ints[d, r * INTS + 1], :, columns
                ].astype(jnp.float32)
                value = jnp.where(tile_row < live, value, 0.0)
                made[d * bucket + r, :, columns] = value.astype(jnp.bfloat16)
            return carry

        lax.fori_loop(0, chan_count, to_one, 0)
        outgoing[i].start()
    for copy in outgoing:
        copy.wait()


def recouple(live_rows, src_map, sixj, tiles, chan_count, chans_dev, chunks=4):
    slots = tiles.shape[0]
    sizes = (chan_count, chans_dev, slots // chans_dev, src_map.shape[2], chunks)
    table = jax.ShapeDtypeStruct((chan_count, LANES), jnp.int32)
    whole = lambda shape: pl.BlockSpec(shape, lambda *_: (0,) * len(shape))
    return pl.pallas_call(
        functools.partial(recouple_kernel, sizes),
        grid_spec=pltpu.PrefetchScalarGridSpec(
            num_scalar_prefetch=1,
            grid=(1,),
            in_specs=[any_spec()] * 3,
            out_specs=[any_spec(), whole(table.shape), whole(table.shape), whole((TILE, LANES))],
            scratch_shapes=[
                pltpu.VMEM(tiles.shape, tiles.dtype),
                pltpu.VMEM(tiles.shape, tiles.dtype),
                pltpu.VMEM(src_map.shape, jnp.int32),
                pltpu.VMEM(sixj.shape, jnp.float32),
                pltpu.VMEM((2, chans_dev, src_map.shape[1], LANES), jnp.int32),
                pltpu.VMEM((2, chans_dev, src_map.shape[1], LANES), jnp.float32),
                pltpu.SMEM(table.shape, jnp.int32),
                pltpu.SMEM(table.shape, jnp.float32),
                pltpu.SemaphoreType.DMA((chunks,)),
                pltpu.SemaphoreType.DMA((chunks,)),
                pltpu.SemaphoreType.DMA((4,)),
            ],
        ),
        out_shape=[
            jax.ShapeDtypeStruct(tiles.shape, tiles.dtype),
            table,
            jax.ShapeDtypeStruct(table.shape, jnp.float32),
            jax.ShapeDtypeStruct((TILE, LANES), jnp.int32),
        ],
        compiler_params=params(60),
    )(live_rows, src_map, sixj, tiles)


def product_kernel(
    start, block, arrival_ref, x_ref, w_ref, out_ref, rows, w_held, made, x_sem, w_sem, out_sem
):
    chans_dev, _, columns = w_ref.shape
    slots = x_ref.shape[0]
    part = slots // chans_dev
    steps = out_ref.shape[2] // block
    depth = w_held.shape[0]

    def x_copy(j, c):
        return pltpu.make_async_copy(x_ref.at[arrival_ref[0, j]], rows.at[j], x_sem.at[c])

    def w_copy(n, c):
        slot = lax.rem(n * chans_dev + c, depth)
        at = pl.ds(pl.multiple_of(start + n * block, block), block)
        return pltpu.make_async_copy(w_ref.at[c, :, at], w_held.at[slot], w_sem.at[slot])

    def out_copy(n):
        at = pl.ds(pl.multiple_of(n * block, block), block)
        return pltpu.make_async_copy(made.at[:, :, at], out_ref.at[:, :, at], out_sem.at[n])

    def each(c, action):
        def one(j, carry):
            action(x_copy(j, c))
            return carry

        lax.fori_loop(c * part, (c + 1) * part, one, 0, unroll=8)

    for c in range(chans_dev):
        w_copy(0, c).start()
        each(c, lambda copy: copy.start())
    for k in range(chans_dev, min(depth, steps * chans_dev)):
        w_copy(k // chans_dev, k % chans_dev).start()

    def step(n, first):
        at = pl.ds(pl.multiple_of(n * block, block), block)
        for c in range(chans_dev):
            if first:
                each(c, lambda copy: copy.wait())
            w_copy(n, c).wait()
            left = rows[pl.ds(c * part, part)].reshape(part * TILE, columns)
            slot = lax.rem(n * chans_dev + c, depth)
            result = jnp.dot(left, w_held[slot], preferred_element_type=jnp.float32)
            result = result.astype(jnp.bfloat16).reshape(part, TILE, block)
            for i in range(part):
                made[arrival_ref[0, c * part + i], :, at] = result[i]

            @pl.when(n + depth // chans_dev < steps)
            def _():
                w_copy(n + depth // chans_dev, c).start()

        out_copy(n).start()

    step(jnp.int32(0), True)

    def body(n, carry):
        step(n, False)
        return carry

    lax.fori_loop(1, steps, body, 0)
    for n in range(steps):
        out_copy(n).wait()


def product(arrival, x, w, start, width, block=256, depth=24):
    chans_dev, columns, _ = w.shape
    depth = min(depth, chans_dev * (width // block))
    made = jax.ShapeDtypeStruct(x.shape[:2] + (width,), x.dtype)
    return pl.pallas_call(
        functools.partial(product_kernel, start, block),
        grid_spec=pltpu.PrefetchScalarGridSpec(
            num_scalar_prefetch=1,
            grid=(1,),
            in_specs=[any_spec(), any_spec()],
            out_specs=any_spec(),
            scratch_shapes=[
                pltpu.VMEM(x.shape, x.dtype),
                pltpu.VMEM((depth, columns, block), w.dtype),
                pltpu.VMEM(made.shape, x.dtype),
                pltpu.SemaphoreType.DMA((chans_dev,)),
                pltpu.SemaphoreType.DMA((depth,)),
                pltpu.SemaphoreType.DMA((width // block,)),
            ],
        ),
        out_shape=made,
        compiler_params=params(60),
    )(arrival, x, w)


def finish_kernel(
    bucket, chunks, ints_ref, coefs_ref, back_ref, pair_ref, out_ref, energy_ref,
    back, pair, made, slot_of, weight_of, back_sem, pair_sem, out_sem,
):
    slots = back.shape[0]
    back_in = column_copies(back_ref, back, back_sem, chunks)
    pair_in = column_copies(pair_ref, pair, pair_sem, chunks)
    outgoing = column_copies(made, out_ref, out_sem, chunks)
    for i in range(chunks):
        back_in[i].start()
        pair_in[i].start()

    def invert(d, carry):
        for r in range(bucket):
            for term in range(2):
                g = ints_ref[d, r * INTS + term]
                slot_of[term, g] = d * bucket + r
                weight_of[term, g] = coefs_ref[d, r * COEFS + term]
        return carry

    lax.fori_loop(0, slots // bucket, invert, 0)
    width = back.shape[2] // chunks
    total = jnp.zeros((TILE, width), jnp.float32)
    for i in range(chunks):
        back_in[i].wait()
        pair_in[i].wait()
        columns = pl.ds(i * width, width)

        def one(g, total):
            value = weight_of[0, g] * back[slot_of[0, g], :, columns].astype(jnp.float32)
            value = value + weight_of[1, g] * back[slot_of[1, g], :, columns].astype(jnp.float32)
            made[g, :, columns] = value.astype(jnp.bfloat16)
            return total + value * pair[g, :, columns].astype(jnp.float32)

        total = lax.fori_loop(0, slots, one, total, unroll=8)
        outgoing[i].start()
    total = jnp.sum(jnp.sum(total, axis=0, keepdims=True), axis=1, keepdims=True)
    energy_ref[...] = jnp.broadcast_to(total, energy_ref.shape)
    for copy in outgoing:
        copy.wait()


def finish(ints, coefs, back, pair, copies, chunks=4):
    slots = back.shape[0]
    bucket = slots // ints.shape[0]
    return pl.pallas_call(
        functools.partial(finish_kernel, bucket, chunks),
        grid_spec=pltpu.PrefetchScalarGridSpec(
            num_scalar_prefetch=2,
            grid=(1,),
            in_specs=[any_spec(), any_spec()],
            out_specs=[any_spec(), pl.BlockSpec((copies, LANES), lambda *_: (0, 0))],
            scratch_shapes=[
                pltpu.VMEM(back.shape, back.dtype),
                pltpu.VMEM(back.shape, back.dtype),
                pltpu.VMEM(back.shape, back.dtype),
                pltpu.SMEM((2, slots), jnp.int32),
                pltpu.SMEM((2, slots), jnp.float32),
                pltpu.SemaphoreType.DMA((chunks,)),
                pltpu.SemaphoreType.DMA((chunks,)),
                pltpu.SemaphoreType.DMA((chunks,)),
            ],
        ),
        out_shape=[
            jax.ShapeDtypeStruct(back.shape, back.dtype),
            jax.ShapeDtypeStruct((copies, LANES), jnp.float32),
        ],
        compiler_params=params(56),
    )(ints, coefs, back, pair)


def exchange(tiles, chan_count):
    parts = tiles.reshape((chan_count, -1) + tiles.shape[1:])
    return lax.all_to_all(parts, "chan", 0, 0, tiled=True).reshape(tiles.shape)


def on_device(pp_amps, ph_coupling, pp_coupling, sixj, src_map, live_rows):
    chan_count = lax.axis_size("chan")
    blk_count = lax.axis_size("blk")
    chans_dev, rows_dev, columns = pp_amps.shape
    slots = chans_dev * rows_dev // TILE
    own_tiles = pp_amps.reshape(slots, TILE, columns)
    pair_tiles = pp_coupling.reshape(slots, TILE, columns)
    sent, ints, coefs, arrival = recouple(
        live_rows, src_map, sixj, own_tiles, chan_count, chans_dev
    )
    got = exchange(sent, chan_count)
    back = exchange(product(arrival, got, ph_coupling, 0, columns, 512, 12), chan_count)
    cycle_pp, partial = finish(ints, coefs, back, pair_tiles, chan_count * blk_count)
    parts = lax.all_to_all(partial, ("chan", "blk"), 0, 0, tiled=True)
    energy = jnp.sum(parts[:, 0]) / (columns * math.sqrt(chan_count * chans_dev))
    return (cycle_pp.reshape(pp_amps.shape), energy)


def solution(mesh):
    in_specs = (
        P("chan", "blk", None),
        P("chan", None, None),
        P("chan", "blk", None),
        P(),
        P(),
        P(),
    )
    out_specs = (P("chan", "blk", None), P())
    return jax.shard_map(
        on_device, mesh=mesh, in_specs=in_specs, out_specs=out_specs, check_vma=False
    )
```

```python
import functools
import math

import jax
import jax.numpy as jnp
from jax import lax
from jax.experimental import pallas as pl
from jax.experimental.pallas import tpu as pltpu
from jax.sharding import PartitionSpec as P

TILE = 8
LANES = 128
BITS = 8
LOW = (1 << BITS) - 1
WIDTHS = (1024, 2048)


def params(mib):
    return pltpu.CompilerParams(vmem_limit_bytes=mib * 1024 * 1024)


def hbm_spec():
    return pl.BlockSpec(memory_space=pltpu.HBM)


def column_copies(source, target, sems, count):
    width = source.shape[2] // count
    return [
        pltpu.make_async_copy(
            source.at[:, :, pl.ds(i * width, width)], target.at[:, :, pl.ds(i * width, width)], sems.at[i]
        )
        for i in range(count)
    ]


def floor_div(values, number):
    return jnp.floor((values.astype(jnp.float32) + 0.5) * (1.0 / number)).astype(jnp.int32)


def recouple_kernel(
    sizes, live_hbm, map_hbm, sixj_hbm, tiles_ref, send_ref, ints_ref, coefs_ref, arrival_ref,
    held, made, live_ref, map_ref, sixj_ref, map_buffer, sixj_buffer, ints, coefs, in_sem, out_sem, table_sem,
):
    chan_count, chans_dev, tiles_dev, all_tiles, chunks = sizes
    slots = chans_dev * tiles_dev
    bucket = slots // chan_count
    incoming = column_copies(tiles_ref, held, in_sem, chunks)
    outgoing = column_copies(made, send_ref, out_sem, chunks)
    from_hbm = [
        pltpu.make_async_copy(map_hbm, map_ref, table_sem.at[2]),
        pltpu.make_async_copy(sixj_hbm, sixj_ref, table_sem.at[3]),
        pltpu.make_async_copy(live_hbm, live_ref, table_sem.at[4]),
    ]
    for copy in from_hbm + incoming[:1]:
        copy.start()

    me = lax.axis_index("chan")
    blk = lax.axis_index("blk")
    lane = lax.broadcasted_iota(jnp.int32, (chan_count, LANES), 1)

    def slab(ref, buffer, term):
        whole = None
        for c in range(chans_dev):
            shift = lax.rem((c - blk) * tiles_dev + all_tiles, all_tiles)
            buffer[term, c] = pltpu.roll(ref[term], shift, axis=1)[:, :LANES]
            rows = buffer[term, c, pl.ds(c, chan_count, stride=chans_dev), :]
            whole = rows if c == 0 else jnp.where(lane < c * tiles_dev, whole, rows)
        return whole

    for copy in from_hbm:
        copy.wait()
    source = None
    local = []
    for term in range(2):
        entry = slab(map_ref, map_buffer, term)
        channel = floor_div(entry, all_tiles)
        owner = floor_div(channel, chans_dev)
        tile = entry - channel * all_tiles - blk * tiles_dev
        local.append((channel - owner * chans_dev) * tiles_dev + tile)
        source = owner if source is None else source
    weight = [slab(sixj_ref, sixj_buffer, term) for term in range(2)]

    mine = (lane < slots) & (source == me)
    at = lax.broadcasted_iota(jnp.int32, (LANES, LANES), 0)
    to = lax.broadcasted_iota(jnp.int32, (LANES, LANES), 1)
    upto = (at <= to).astype(jnp.bfloat16)
    rank = jnp.dot(mine.astype(jnp.bfloat16), upto, preferred_element_type=jnp.float32)
    rank = rank.astype(jnp.int32) - 1
    packed = local[0] + (local[1] << BITS) + (lane << 2 * BITS)
    int_table = jnp.zeros((chan_count, LANES), jnp.int32)
    coef_table = jnp.zeros((chan_count, LANES), jnp.float32)
    for r in range(bucket):
        chosen = mine & (rank == r)
        value = jnp.sum(jnp.where(chosen, packed, 0), axis=1, keepdims=True)
        int_table = jnp.where(lane == r, value, int_table)
        for term, values in enumerate(weight):
            value = jnp.sum(jnp.where(chosen, values, 0.0), axis=1, keepdims=True)
            coef_table = jnp.where(lane == 2 * r + term, value, coef_table)
    ints_ref[...] = int_table
    coefs_ref[...] = coef_table
    to_smem = [
        pltpu.make_async_copy(ints_ref, ints, table_sem.at[0]),
        pltpu.make_async_copy(coefs_ref, coefs, table_sem.at[1]),
    ]
    for copy in to_smem + incoming[1:]:
        copy.start()

    row = lax.broadcasted_iota(jnp.int32, (chan_count, LANES), 0)
    own = jnp.sum(jnp.where(row == me, source, 0), axis=0, keepdims=True)
    across = jnp.broadcast_to(own, (LANES, LANES))
    earlier = (across.T == across) & (at < to)
    arrival = own * bucket + jnp.sum(earlier.astype(jnp.int32), axis=0, keepdims=True)
    arrival_ref[...] = jnp.broadcast_to(arrival, arrival_ref.shape)

    for copy in to_smem:
        copy.wait()
    width = held.shape[2] // chunks
    tile_row = lax.broadcasted_iota(jnp.int32, (TILE, width), 0)
    for i in range(chunks):
        incoming[i].wait()
        columns = pl.ds(i * width, width)

        def to_one(d, carry):
            for r in range(bucket):
                entry = ints[d, r]
                slot = entry >> 2 * BITS
                c = sum((slot >= k * tiles_dev).astype(jnp.int32) for k in range(1, chans_dev))
                first_row = (blk * tiles_dev + slot - c * tiles_dev) * TILE
                live = live_ref[d * chans_dev + c] - first_row
                first = held[entry & LOW, :, columns].astype(jnp.float32)
                second = held[(entry >> BITS) & LOW, :, columns].astype(jnp.float32)
                value = coefs[d, 2 * r] * first + coefs[d, 2 * r + 1] * second
                value = jnp.where(tile_row < live, value, 0.0)
                made[d * bucket + r, :, columns] = value.astype(jnp.bfloat16)
            return carry

        lax.fori_loop(0, chan_count, to_one, 0)
        outgoing[i].start()
    for copy in outgoing:
        copy.wait()


def recouple(live_rows, src_map, sixj, tiles, chan_count, chans_dev, chunks=3):
    slots = tiles.shape[0]
    sizes = (chan_count, chans_dev, slots // chans_dev, src_map.shape[2], chunks)
    table = jax.ShapeDtypeStruct((chan_count, LANES), jnp.int32)
    return pl.pallas_call(
        functools.partial(recouple_kernel, sizes),
        grid_spec=pltpu.PrefetchScalarGridSpec(
            num_scalar_prefetch=0,
            in_specs=[hbm_spec()] * 4,
            out_specs=[hbm_spec()] + [pl.BlockSpec(memory_space=pltpu.VMEM)] * 3,
            scratch_shapes=[
                pltpu.VMEM(tiles.shape, tiles.dtype),
                pltpu.VMEM(tiles.shape, tiles.dtype),
                pltpu.SMEM(live_rows.shape, jnp.int32),
                pltpu.VMEM(src_map.shape, jnp.int32),
                pltpu.VMEM(sixj.shape, jnp.float32),
                pltpu.VMEM((2, chans_dev, src_map.shape[1], LANES), jnp.int32),
                pltpu.VMEM((2, chans_dev, src_map.shape[1], LANES), jnp.float32),
                pltpu.SMEM(table.shape, jnp.int32),
                pltpu.SMEM(table.shape, jnp.float32),
                pltpu.SemaphoreType.DMA((chunks,)),
                pltpu.SemaphoreType.DMA((chunks,)),
                pltpu.SemaphoreType.DMA((5,)),
            ],
        ),
        out_shape=[
            jax.ShapeDtypeStruct(tiles.shape, tiles.dtype),
            table,
            jax.ShapeDtypeStruct(table.shape, jnp.float32),
            jax.ShapeDtypeStruct((TILE, LANES), jnp.int32),
        ],
        compiler_params=params(63),
    )(live_rows, src_map, sixj, tiles)


def product_kernel(
    start, block, arrival_hbm, x_ref, w_ref, out_ref,
    arrival_ref, rows, w_held, made, x_sem, w_sem, out_sem, table_sem,
):
    chans_dev, _, columns = w_ref.shape
    slots = x_ref.shape[0]
    part = slots // chans_dev
    steps = out_ref.shape[2] // block
    depth = w_held.shape[0]

    def x_copy(j, c):
        return pltpu.make_async_copy(x_ref.at[arrival_ref[0, j]], rows.at[j], x_sem.at[c])

    def w_copy(n, c):
        slot = lax.rem(n * chans_dev + c, depth)
        at = pl.ds(pl.multiple_of(start + n * block, block), block)
        return pltpu.make_async_copy(w_ref.at[c, :, at], w_held.at[slot], w_sem.at[slot])

    def out_copy(n):
        at = pl.ds(pl.multiple_of(n * block, block), block)
        return pltpu.make_async_copy(made.at[:, :, at], out_ref.at[:, :, at], out_sem.at[n])

    def each(c, action):
        def one(j, carry):
            action(x_copy(j, c))
            return carry

        lax.fori_loop(c * part, (c + 1) * part, one, 0, unroll=8)

    table = pltpu.make_async_copy(arrival_hbm, arrival_ref, table_sem)
    table.start()
    w_copy(0, 0).start()
    table.wait()
    for c in range(chans_dev):
        if c:
            w_copy(0, c).start()
        each(c, lambda copy: copy.start())
    for k in range(chans_dev, min(depth, steps * chans_dev)):
        w_copy(k // chans_dev, k % chans_dev).start()

    def step(n, first):
        at = pl.ds(pl.multiple_of(n * block, block), block)
        for c in range(chans_dev):
            if first:
                each(c, lambda copy: copy.wait())
            w_copy(n, c).wait()
            left = rows[pl.ds(c * part, part)].reshape(part * TILE, columns)
            slot = lax.rem(n * chans_dev + c, depth)
            result = jnp.dot(left, w_held[slot], preferred_element_type=jnp.float32)
            result = result.astype(jnp.bfloat16).reshape(part, TILE, block)
            for i in range(part):
                made[arrival_ref[0, c * part + i], :, at] = result[i]

            @pl.when(n + depth // chans_dev < steps)
            def _():
                w_copy(n + depth // chans_dev, c).start()

        out_copy(n).start()

    step(jnp.int32(0), True)

    def body(n, carry):
        step(n, False)
        return carry

    lax.fori_loop(1, steps, body, 0)
    for n in range(steps):
        out_copy(n).wait()


def product(arrival, x, w, start, width, block=512, depth=12):
    chans_dev, columns, _ = w.shape
    depth = min(depth, chans_dev * (width // block))
    made = jax.ShapeDtypeStruct(x.shape[:2] + (width,), x.dtype)
    return pl.pallas_call(
        functools.partial(product_kernel, start, block),
        grid_spec=pltpu.PrefetchScalarGridSpec(
            num_scalar_prefetch=0,
            in_specs=[hbm_spec()] * 3,
            out_specs=hbm_spec(),
            scratch_shapes=[
                pltpu.SMEM(arrival.shape, jnp.int32),
                pltpu.VMEM(x.shape, x.dtype),
                pltpu.VMEM((depth, columns, block), w.dtype),
                pltpu.VMEM(made.shape, x.dtype),
                pltpu.SemaphoreType.DMA((chans_dev,)),
                pltpu.SemaphoreType.DMA((depth,)),
                pltpu.SemaphoreType.DMA((width // block,)),
                pltpu.SemaphoreType.DMA,
            ],
        ),
        out_shape=made,
        compiler_params=params(63),
        cost_estimate=pl.CostEstimate(
            flops=2 * x.size * width,
            bytes_accessed=2 * (x.size + made.size + chans_dev * columns * width),
            transcendentals=0,
        ),
    )(arrival, x, w)


def finish_kernel(start, chunks, adds, writes, ints_hbm, coefs_hbm, back_ref, pair_ref, *refs):
    refs = list(refs)
    if start and writes:
        refs.pop(0)
    before_ref = refs.pop(0) if start and adds else None
    out_ref = refs.pop(0) if writes else None
    energy_ref = refs.pop(0) if adds else None
    ints_ref, coefs_ref, back, pair, made, slot_of, weight_of, back_sem, pair_sem, out_sem, table_sem = refs
    slots, _, columns = back.shape
    bucket = slots // ints_ref.shape[0]
    here = pl.ds(start, columns)
    incoming = [column_copies(back_ref, back, back_sem, chunks)]
    if adds:
        incoming.append(column_copies(pair_ref.at[:, :, here], pair, pair_sem, chunks))
    outgoing = column_copies(made, out_ref.at[:, :, here], out_sem, chunks) if writes else []
    tables = [
        pltpu.make_async_copy(ints_hbm, ints_ref, table_sem.at[0]),
        pltpu.make_async_copy(coefs_hbm, coefs_ref, table_sem.at[1]),
    ]
    for copies in [tables] + list(zip(*incoming)):
        for copy in copies:
            copy.start()
    for copy in tables:
        copy.wait()

    def invert(d, carry):
        for r in range(bucket):
            entry = ints_ref[d, r]
            for term in range(2):
                g = (entry >> (term * BITS)) & LOW
                slot_of[term, g] = d * bucket + r
                weight_of[term, g] = coefs_ref[d, 2 * r + term]
        return carry

    lax.fori_loop(0, slots // bucket, invert, 0)
    width = columns // chunks
    total = jnp.zeros((TILE, width), jnp.float32)
    for i in range(chunks):
        for copies in incoming:
            copies[i].wait()
        at = pl.ds(i * width, width)

        def one(g, total):
            value = weight_of[0, g] * back[slot_of[0, g], :, at].astype(jnp.float32)
            value = value + weight_of[1, g] * back[slot_of[1, g], :, at].astype(jnp.float32)
            value = value.astype(jnp.bfloat16)
            if writes:
                made[g, :, at] = value
            if adds:
                total = total + value.astype(jnp.float32) * pair[g, :, at].astype(jnp.float32)
            return total

        total = lax.fori_loop(0, slots, one, total, unroll=8)
        if writes:
            outgoing[i].start()
    if adds:
        total = jnp.sum(jnp.sum(total, axis=0, keepdims=True), axis=1, keepdims=True)
        total = jnp.broadcast_to(total, energy_ref.shape)
        energy_ref[...] = total + before_ref[...] if start else total
    for copy in outgoing:
        copy.wait()


def finish(ints, coefs, back, pair, start, written, added, copies, chunks, adds=True, writes=True):
    energy = pl.BlockSpec(memory_space=pltpu.VMEM)
    again, more = bool(start and writes), bool(start and adds)
    outs = [(hbm_spec(), jax.ShapeDtypeStruct(pair.shape, pair.dtype))] * writes
    outs = outs + [(energy, jax.ShapeDtypeStruct((copies, LANES), jnp.float32))] * adds
    return pl.pallas_call(
        functools.partial(finish_kernel, start, chunks, adds, writes),
        grid_spec=pltpu.PrefetchScalarGridSpec(
            num_scalar_prefetch=0,
            in_specs=[hbm_spec()] * (4 + again) + [energy] * more,
            out_specs=[spec for spec, _ in outs],
            scratch_shapes=[
                pltpu.SMEM(ints.shape, jnp.int32),
                pltpu.SMEM(coefs.shape, jnp.float32),
                pltpu.VMEM(back.shape, back.dtype),
                pltpu.VMEM(back.shape, back.dtype),
                pltpu.VMEM(back.shape, back.dtype),
                pltpu.SMEM((2, back.shape[0]), jnp.int32),
                pltpu.SMEM((2, back.shape[0]), jnp.float32),
                pltpu.SemaphoreType.DMA((chunks,)),
                pltpu.SemaphoreType.DMA((chunks,)),
                pltpu.SemaphoreType.DMA((chunks,)),
                pltpu.SemaphoreType.DMA((2,)),
            ],
        ),
        out_shape=[shape for _, shape in outs],
        input_output_aliases={4: 0} if again else {},
        compiler_params=params(63),
        cost_estimate=pl.CostEstimate(
            flops=6 * back.size, bytes_accessed=6 * back.size, transcendentals=0
        ),
    )(ints, coefs, back, pair, *[written] * again, *[added] * more)


def exchange(tiles, chan_count):
    parts = tiles.reshape((chan_count, -1) + tiles.shape[1:])
    return lax.all_to_all(parts, "chan", 0, 0, tiled=True).reshape(tiles.shape)


def on_device(pp_amps, ph_coupling, pp_coupling, sixj, src_map, live_rows):
    chan_count = lax.axis_size("chan")
    blk_count = lax.axis_size("blk")
    chans_dev, rows_dev, columns = pp_amps.shape
    slots = chans_dev * rows_dev // TILE
    own_tiles = pp_amps.reshape(slots, TILE, columns)
    pair_tiles = pp_coupling.reshape(slots, TILE, columns)
    sent, ints, coefs, arrival = recouple(
        live_rows, src_map, sixj, own_tiles, chan_count, chans_dev
    )
    got = exchange(sent, chan_count)
    cycle_pp = partial = None
    start = 0
    for width in WIDTHS:
        made = product(arrival, got, ph_coupling, start, width)
        back = exchange(made, chan_count)
        chunks = max(1, 4 * width // columns)
        call = functools.partial(
            finish, ints, coefs, back, pair_tiles, start, cycle_pp, partial, chan_count * blk_count, chunks
        )
        start += width
        if start < columns:
            cycle_pp, partial = call()
        else:
            (partial,) = call(writes=False)
            (cycle_pp,) = call(adds=False)
    parts = lax.all_to_all(partial, ("chan", "blk"), 0, 0, tiled=True)
    energy = jnp.sum(parts[:, 0]) / (columns * math.sqrt(chan_count * chans_dev))
    return (cycle_pp.reshape(pp_amps.shape), energy)


def solution(mesh):
    in_specs = (
        P("chan", "blk", None),
        P("chan", None, None),
        P("chan", "blk", None),
        P(),
        P(),
        P(),
    )
    out_specs = (P("chan", "blk", None), P())
    return jax.shard_map(
        on_device, mesh=mesh, in_specs=in_specs, out_specs=out_specs, check_vma=False
    )
```

```python
import functools
import math

import jax
import jax.numpy as jnp
from jax import lax
from jax.experimental import pallas as pl
from jax.experimental.pallas import tpu as pltpu
from jax.sharding import PartitionSpec as P

TILE = 8
LANES = 128
BITS = 8
LOW = (1 << BITS) - 1
WIDTHS = (1024, 2048)


def params(mib):
    return pltpu.CompilerParams(vmem_limit_bytes=mib * 1024 * 1024)


def hbm_spec():
    return pl.BlockSpec(memory_space=pltpu.HBM)


def column_copies(source, target, sems, count):
    width = source.shape[2] // count
    return [
        pltpu.make_async_copy(
            source.at[:, :, pl.ds(i * width, width)], target.at[:, :, pl.ds(i * width, width)], sems.at[i]
        )
        for i in range(count)
    ]


def floor_div(values, number):
    return jnp.floor((values.astype(jnp.float32) + 0.5) * (1.0 / number)).astype(jnp.int32)


def recouple_kernel(
    sizes, live_hbm, map_hbm, sixj_hbm, tiles_ref, send_ref, ints_ref, coefs_ref, arrival_ref,
    held, made, live_ref, map_ref, sixj_ref, map_buffer, sixj_buffer, ints, coefs, in_sem, out_sem, table_sem,
):
    chan_count, chans_dev, tiles_dev, all_tiles, chunks = sizes
    slots = chans_dev * tiles_dev
    bucket = slots // chan_count
    incoming = column_copies(tiles_ref, held, in_sem, chunks)
    outgoing = column_copies(made, send_ref, out_sem, chunks)
    from_hbm = [
        pltpu.make_async_copy(map_hbm, map_ref, table_sem.at[2]),
        pltpu.make_async_copy(sixj_hbm, sixj_ref, table_sem.at[3]),
        pltpu.make_async_copy(live_hbm, live_ref, table_sem.at[4]),
    ]
    for copy in from_hbm + incoming[:1]:
        copy.start()

    me = lax.axis_index("chan")
    blk = lax.axis_index("blk")
    lane = lax.broadcasted_iota(jnp.int32, (chan_count, LANES), 1)

    def slab(ref, buffer, term):
        whole = None
        for c in range(chans_dev):
            shift = lax.rem((c - blk) * tiles_dev + all_tiles, all_tiles)
            buffer[term, c] = pltpu.roll(ref[term], shift, axis=1)[:, :LANES]
            rows = buffer[term, c, pl.ds(c, chan_count, stride=chans_dev), :]
            whole = rows if c == 0 else jnp.where(lane < c * tiles_dev, whole, rows)
        return whole

    for copy in from_hbm:
        copy.wait()
    for copy in incoming[1:]:
        copy.start()
    source = None
    local = []
    for term in range(2):
        entry = slab(map_ref, map_buffer, term)
        channel = floor_div(entry, all_tiles)
        owner = floor_div(channel, chans_dev)
        tile = entry - channel * all_tiles - blk * tiles_dev
        local.append((channel - owner * chans_dev) * tiles_dev + tile)
        source = owner if source is None else source
    weight = [slab(sixj_ref, sixj_buffer, term) for term in range(2)]

    mine = (lane < slots) & (source == me)
    at = lax.broadcasted_iota(jnp.int32, (LANES, LANES), 0)
    to = lax.broadcasted_iota(jnp.int32, (LANES, LANES), 1)
    upto = (at <= to).astype(jnp.bfloat16)
    rank = jnp.dot(mine.astype(jnp.bfloat16), upto, preferred_element_type=jnp.float32)
    rank = rank.astype(jnp.int32) - 1
    packed = local[0] + (local[1] << BITS) + (lane << 2 * BITS)
    int_table = jnp.zeros((chan_count, LANES), jnp.int32)
    coef_table = jnp.zeros((chan_count, LANES), jnp.float32)
    for r in range(bucket):
        chosen = mine & (rank == r)
        value = jnp.sum(jnp.where(chosen, packed, 0), axis=1, keepdims=True)
        int_table = jnp.where(lane == r, value, int_table)
        for term, values in enumerate(weight):
            value = jnp.sum(jnp.where(chosen, values, 0.0), axis=1, keepdims=True)
            coef_table = jnp.where(lane == 2 * r + term, value, coef_table)
    ints_ref[...] = int_table
    coefs_ref[...] = coef_table
    to_smem = [
        pltpu.make_async_copy(ints_ref, ints, table_sem.at[0]),
        pltpu.make_async_copy(coefs_ref, coefs, table_sem.at[1]),
    ]
    for copy in to_smem:
        copy.start()

    row = lax.broadcasted_iota(jnp.int32, (chan_count, LANES), 0)
    own = jnp.sum(jnp.where(row == me, source, 0), axis=0, keepdims=True)
    across = jnp.broadcast_to(own, (LANES, LANES))
    earlier = (across.T == across) & (at < to)
    arrival = own * bucket + jnp.sum(earlier.astype(jnp.int32), axis=0, keepdims=True)
    arrival_ref[...] = jnp.broadcast_to(arrival, arrival_ref.shape)

    for copy in to_smem:
        copy.wait()
    width = held.shape[2] // chunks
    tile_row = lax.broadcasted_iota(jnp.int32, (TILE, LANES), 0)
    for i in range(chunks):
        incoming[i].wait()
        columns = pl.ds(i * width, width)

        def to_one(d, carry):
            for r in range(bucket):
                entry = ints[d, r]
                slot = entry >> 2 * BITS
                c = sum((slot >= k * tiles_dev).astype(jnp.int32) for k in range(1, chans_dev))
                first_row = (blk * tiles_dev + slot - c * tiles_dev) * TILE
                live = live_ref[d * chans_dev + c] - first_row
                first = held[entry & LOW, :, columns].astype(jnp.float32)
                second = held[(entry >> BITS) & LOW, :, columns].astype(jnp.float32)
                keep = tile_row < live
                scale = [
                    jnp.tile(jnp.where(keep, coefs[d, 2 * r + term], 0.0), (1, width // LANES))
                    for term in range(2)
                ]
                value = scale[0] * first + scale[1] * second
                made[d * bucket + r, :, columns] = value.astype(jnp.bfloat16)
            return carry

        lax.fori_loop(0, chan_count, to_one, 0, unroll=2)
        outgoing[i].start()
    for copy in outgoing:
        copy.wait()


def recouple(live_rows, src_map, sixj, tiles, chan_count, chans_dev, chunks=3):
    slots = tiles.shape[0]
    sizes = (chan_count, chans_dev, slots // chans_dev, src_map.shape[2], chunks)
    table = jax.ShapeDtypeStruct((chan_count, LANES), jnp.int32)
    return pl.pallas_call(
        functools.partial(recouple_kernel, sizes),
        grid_spec=pltpu.PrefetchScalarGridSpec(
            num_scalar_prefetch=0,
            in_specs=[hbm_spec()] * 4,
            out_specs=[hbm_spec()] + [pl.BlockSpec(memory_space=pltpu.VMEM)] * 3,
            scratch_shapes=[
                pltpu.VMEM(tiles.shape, tiles.dtype),
                pltpu.VMEM(tiles.shape, tiles.dtype),
                pltpu.SMEM(live_rows.shape, jnp.int32),
                pltpu.VMEM(src_map.shape, jnp.int32),
                pltpu.VMEM(sixj.shape, jnp.float32),
                pltpu.VMEM((2, chans_dev, src_map.shape[1], LANES), jnp.int32),
                pltpu.VMEM((2, chans_dev, src_map.shape[1], LANES), jnp.float32),
                pltpu.SMEM(table.shape, jnp.int32),
                pltpu.SMEM(table.shape, jnp.float32),
                pltpu.SemaphoreType.DMA((chunks,)),
                pltpu.SemaphoreType.DMA((chunks,)),
                pltpu.SemaphoreType.DMA((5,)),
            ],
        ),
        out_shape=[
            jax.ShapeDtypeStruct(tiles.shape, tiles.dtype),
            table,
            jax.ShapeDtypeStruct(table.shape, jnp.float32),
            jax.ShapeDtypeStruct((TILE, LANES), jnp.int32),
        ],
        compiler_params=params(63),
    )(live_rows, src_map, sixj, tiles)


def product_kernel(
    start, block, arrival_hbm, x_ref, w_ref, out_ref,
    arrival_ref, rows, w_held, made, x_sem, w_sem, out_sem, table_sem,
):
    chans_dev, _, columns = w_ref.shape
    slots = x_ref.shape[0]
    part = slots // chans_dev
    steps = out_ref.shape[2] // block
    depth = w_held.shape[0]

    def x_copy(j, c):
        return pltpu.make_async_copy(x_ref.at[arrival_ref[0, j]], rows.at[j], x_sem.at[c])

    def w_copy(n, c):
        slot = lax.rem(n * chans_dev + c, depth)
        at = pl.ds(pl.multiple_of(start + n * block, block), block)
        return pltpu.make_async_copy(w_ref.at[c, :, at], w_held.at[slot], w_sem.at[slot])

    def out_copy(n):
        at = pl.ds(pl.multiple_of(n * block, block), block)
        return pltpu.make_async_copy(made.at[:, :, at], out_ref.at[:, :, at], out_sem.at[n])

    def each(c, action):
        def one(j, carry):
            action(x_copy(j, c))
            return carry

        lax.fori_loop(c * part, (c + 1) * part, one, 0, unroll=8)

    table = pltpu.make_async_copy(arrival_hbm, arrival_ref, table_sem)
    table.start()
    w_copy(0, 0).start()
    table.wait()
    for c in range(chans_dev):
        if c:
            w_copy(0, c).start()
        each(c, lambda copy: copy.start())
    for k in range(chans_dev, min(depth, steps * chans_dev)):
        w_copy(k // chans_dev, k % chans_dev).start()

    def step(n, first):
        at = pl.ds(pl.multiple_of(n * block, block), block)
        for c in range(chans_dev):
            if first:
                each(c, lambda copy: copy.wait())
            w_copy(n, c).wait()
            left = rows[pl.ds(c * part, part)].reshape(part * TILE, columns)
            slot = lax.rem(n * chans_dev + c, depth)
            result = jnp.dot(left, w_held[slot], preferred_element_type=jnp.float32)
            result = result.astype(jnp.bfloat16).reshape(part, TILE, block)
            for i in range(part):
                made[arrival_ref[0, c * part + i], :, at] = result[i]

            @pl.when(n + depth // chans_dev < steps)
            def _():
                w_copy(n + depth // chans_dev, c).start()

        out_copy(n).start()

    step(jnp.int32(0), True)

    def body(n, carry):
        step(n, False)
        return carry

    lax.fori_loop(1, steps, body, 0)
    for n in range(steps):
        out_copy(n).wait()


def product(arrival, x, w, start, width, block=512, depth=12):
    chans_dev, columns, _ = w.shape
    depth = min(depth, chans_dev * (width // block))
    made = jax.ShapeDtypeStruct(x.shape[:2] + (width,), x.dtype)
    return pl.pallas_call(
        functools.partial(product_kernel, start, block),
        grid_spec=pltpu.PrefetchScalarGridSpec(
            num_scalar_prefetch=0,
            in_specs=[hbm_spec()] * 3,
            out_specs=hbm_spec(),
            scratch_shapes=[
                pltpu.SMEM(arrival.shape, jnp.int32),
                pltpu.VMEM(x.shape, x.dtype),
                pltpu.VMEM((depth, columns, block), w.dtype),
                pltpu.VMEM(made.shape, x.dtype),
                pltpu.SemaphoreType.DMA((chans_dev,)),
                pltpu.SemaphoreType.DMA((depth,)),
                pltpu.SemaphoreType.DMA((width // block,)),
                pltpu.SemaphoreType.DMA,
            ],
        ),
        out_shape=made,
        compiler_params=params(63),
        cost_estimate=pl.CostEstimate(
            flops=2 * x.size * width,
            bytes_accessed=2 * (x.size + made.size + chans_dev * columns * width),
            transcendentals=0,
        ),
    )(arrival, x, w)


def finish_kernel(start, chunks, adds, writes, ints_hbm, coefs_hbm, back_ref, pair_ref, *refs):
    refs = list(refs)
    if start and writes:
        refs.pop(0)
    before_hbm = refs.pop(0) if start and adds else None
    out_ref = refs.pop(0) if writes else None
    energy_ref = refs.pop(0) if adds else None
    ints_ref, coefs_ref, before_ref, back, pair, made, slot_of, weight_of, back_sem, pair_sem, out_sem, table_sem = refs
    slots, _, columns = back.shape
    bucket = slots // ints_ref.shape[0]
    here = pl.ds(start, columns)
    incoming = [column_copies(back_ref, back, back_sem, chunks)]
    if adds:
        incoming.append(column_copies(pair_ref.at[:, :, here], pair, pair_sem, chunks))
    outgoing = column_copies(made, out_ref.at[:, :, here], out_sem, chunks) if writes else []
    tables = [
        pltpu.make_async_copy(ints_hbm, ints_ref, table_sem.at[0]),
        pltpu.make_async_copy(coefs_hbm, coefs_ref, table_sem.at[1]),
    ]
    if start and adds:
        earlier = pltpu.make_async_copy(before_hbm, before_ref, table_sem.at[2])
        tables.append(earlier)
    for copies in [tables] + list(zip(*incoming)):
        for copy in copies:
            copy.start()
    for copy in tables:
        copy.wait()

    def invert(d, carry):
        for r in range(bucket):
            entry = ints_ref[d, r]
            for term in range(2):
                g = (entry >> (term * BITS)) & LOW
                slot_of[term, g] = d * bucket + r
                weight_of[term, g] = coefs_ref[d, 2 * r + term]
        return carry

    lax.fori_loop(0, slots // bucket, invert, 0)
    width = columns // chunks
    total = jnp.zeros((TILE, width), jnp.float32)
    for i in range(chunks):
        for copies in incoming:
            copies[i].wait()
        at = pl.ds(i * width, width)

        def one(g, total):
            value = weight_of[0, g] * back[slot_of[0, g], :, at].astype(jnp.float32)
            value = value + weight_of[1, g] * back[slot_of[1, g], :, at].astype(jnp.float32)
            value = value.astype(jnp.bfloat16)
            if writes:
                made[g, :, at] = value
            if adds:
                total = total + value.astype(jnp.float32) * pair[g, :, at].astype(jnp.float32)
            return total

        total = lax.fori_loop(0, slots, one, total, unroll=8)
        if writes:
            outgoing[i].start()
    if adds:
        total = jnp.sum(jnp.sum(total, axis=0, keepdims=True), axis=1, keepdims=True)
        total = jnp.broadcast_to(total, energy_ref.shape)
        energy_ref[...] = total + before_ref[0:1, :] if start else total
    for copy in outgoing:
        copy.wait()


def finish(ints, coefs, back, pair, start, written, added, copies, chunks, adds=True, writes=True):
    energy = pl.BlockSpec(memory_space=pltpu.VMEM)
    again, more = bool(start and writes), bool(start and adds)
    outs = [(hbm_spec(), jax.ShapeDtypeStruct(pair.shape, pair.dtype))] * writes
    outs = outs + [(energy, jax.ShapeDtypeStruct((copies, LANES), jnp.float32))] * adds
    return pl.pallas_call(
        functools.partial(finish_kernel, start, chunks, adds, writes),
        grid_spec=pltpu.PrefetchScalarGridSpec(
            num_scalar_prefetch=0,
            in_specs=[hbm_spec()] * (4 + again + more),
            out_specs=[spec for spec, _ in outs],
            scratch_shapes=[
                pltpu.SMEM(ints.shape, jnp.int32),
                pltpu.SMEM(coefs.shape, jnp.float32),
                pltpu.VMEM((TILE, LANES), jnp.float32),
                pltpu.VMEM(back.shape, back.dtype),
                pltpu.VMEM(back.shape, back.dtype),
                pltpu.VMEM(back.shape, back.dtype),
                pltpu.SMEM((2, back.shape[0]), jnp.int32),
                pltpu.SMEM((2, back.shape[0]), jnp.float32),
                pltpu.SemaphoreType.DMA((chunks,)),
                pltpu.SemaphoreType.DMA((chunks,)),
                pltpu.SemaphoreType.DMA((chunks,)),
                pltpu.SemaphoreType.DMA((3,)),
            ],
        ),
        out_shape=[shape for _, shape in outs],
        input_output_aliases={4: 0} if again else {},
        compiler_params=params(63),
        cost_estimate=pl.CostEstimate(
            flops=6 * back.size, bytes_accessed=6 * back.size, transcendentals=0
        ),
    )(ints, coefs, back, pair, *[written] * again, *[added] * more)


def exchange(tiles, chan_count):
    parts = tiles.reshape((chan_count, -1) + tiles.shape[1:])
    return lax.all_to_all(parts, "chan", 0, 0, tiled=True).reshape(tiles.shape)


def on_device(pp_amps, ph_coupling, pp_coupling, sixj, src_map, live_rows):
    chan_count = lax.axis_size("chan")
    blk_count = lax.axis_size("blk")
    chans_dev, rows_dev, columns = pp_amps.shape
    slots = chans_dev * rows_dev // TILE
    own_tiles = pp_amps.reshape(slots, TILE, columns)
    pair_tiles = pp_coupling.reshape(slots, TILE, columns)
    sent, ints, coefs, arrival = recouple(
        live_rows, src_map, sixj, own_tiles, chan_count, chans_dev
    )
    got = exchange(sent, chan_count)
    cycle_pp = partial = None
    start = 0
    for width in WIDTHS:
        made = product(arrival, got, ph_coupling, start, width)
        back = exchange(made, chan_count)
        chunks = max(1, 4 * width // columns)
        last = start + width == columns
        copies = chan_count * blk_count if last else TILE
        call = functools.partial(
            finish, ints, coefs, back, pair_tiles, start, cycle_pp, partial, copies, chunks
        )
        start += width
        if last:
            (partial,) = call(writes=False)
            (cycle_pp,) = call(adds=False)
        else:
            cycle_pp, partial = call()
    parts = lax.all_to_all(partial, ("chan", "blk"), 0, 0, tiled=True)
    energy = jnp.sum(parts[:, 0]) / (columns * math.sqrt(chan_count * chans_dev))
    return (cycle_pp.reshape(pp_amps.shape), energy)


def solution(mesh):
    in_specs = (
        P("chan", "blk", None),
        P("chan", None, None),
        P("chan", "blk", None),
        P(),
        P(),
        P(),
    )
    out_specs = (P("chan", "blk", None), P())
    return jax.shard_map(
        on_device, mesh=mesh, in_specs=in_specs, out_specs=out_specs, check_vma=False
    )
```

```python
import functools
import math

import jax
import jax.numpy as jnp
from jax import lax
from jax.experimental import pallas as pl
from jax.experimental.pallas import tpu as pltpu
from jax.sharding import PartitionSpec as P

TILE = 8
LANES = 128
BITS = 8
LOW = (1 << BITS) - 1
WIDTHS = (1024, 2048)


def params(mib):
    return pltpu.CompilerParams(vmem_limit_bytes=mib * 1024 * 1024)


def hbm_spec():
    return pl.BlockSpec(memory_space=pltpu.HBM)


def column_copies(source, target, sems, count):
    width = source.shape[2] // count
    return [
        pltpu.make_async_copy(
            source.at[:, :, pl.ds(i * width, width)], target.at[:, :, pl.ds(i * width, width)], sems.at[i]
        )
        for i in range(count)
    ]


def floor_div(values, number):
    return jnp.floor((values.astype(jnp.float32) + 0.5) * (1.0 / number)).astype(jnp.int32)


def recouple_kernel(
    sizes, live_hbm, map_hbm, sixj_hbm, tiles_ref, send_ref, ints_ref, coefs_ref, arrival_ref,
    held, made, live_ref, map_ref, sixj_ref, map_buffer, sixj_buffer, ints, coefs, in_sem, out_sem, table_sem,
):
    chan_count, chans_dev, tiles_dev, all_tiles, chunks = sizes
    slots = chans_dev * tiles_dev
    bucket = slots // chan_count
    incoming = column_copies(tiles_ref, held, in_sem, chunks)
    outgoing = column_copies(made, send_ref, out_sem, chunks)
    from_hbm = [
        pltpu.make_async_copy(map_hbm, map_ref, table_sem.at[2]),
        pltpu.make_async_copy(sixj_hbm, sixj_ref, table_sem.at[3]),
        pltpu.make_async_copy(live_hbm, live_ref, table_sem.at[4]),
    ]
    for copy in from_hbm + incoming[:1]:
        copy.start()

    me = lax.axis_index("chan")
    blk = lax.axis_index("blk")
    lane = lax.broadcasted_iota(jnp.int32, (chan_count, LANES), 1)

    def slab(ref, buffer, term):
        whole = None
        for c in range(chans_dev):
            shift = lax.rem((c - blk) * tiles_dev + all_tiles, all_tiles)
            buffer[term, c] = pltpu.roll(ref[term], shift, axis=1)[:, :LANES]
            rows = buffer[term, c, pl.ds(c, chan_count, stride=chans_dev), :]
            whole = rows if c == 0 else jnp.where(lane < c * tiles_dev, whole, rows)
        return whole

    for copy in from_hbm:
        copy.wait()
    for copy in incoming[1:]:
        copy.start()
    source = None
    local = []
    for term in range(2):
        entry = slab(map_ref, map_buffer, term)
        channel = floor_div(entry, all_tiles)
        owner = floor_div(channel, chans_dev)
        tile = entry - channel * all_tiles - blk * tiles_dev
        local.append((channel - owner * chans_dev) * tiles_dev + tile)
        source = owner if source is None else source
    weight = [slab(sixj_ref, sixj_buffer, term) for term in range(2)]

    mine = (lane < slots) & (source == me)
    at = lax.broadcasted_iota(jnp.int32, (LANES, LANES), 0)
    to = lax.broadcasted_iota(jnp.int32, (LANES, LANES), 1)
    upto = (at <= to).astype(jnp.bfloat16)
    rank = jnp.dot(mine.astype(jnp.bfloat16), upto, preferred_element_type=jnp.float32)
    rank = rank.astype(jnp.int32) - 1
    packed = local[0] + (local[1] << BITS) + (lane << 2 * BITS)
    int_table = jnp.zeros((chan_count, LANES), jnp.int32)
    coef_table = jnp.zeros((chan_count, LANES), jnp.float32)
    for r in range(bucket):
        chosen = mine & (rank == r)
        value = jnp.sum(jnp.where(chosen, packed, 0), axis=1, keepdims=True)
        int_table = jnp.where(lane == r, value, int_table)
        for term, values in enumerate(weight):
            value = jnp.sum(jnp.where(chosen, values, 0.0), axis=1, keepdims=True)
            coef_table = jnp.where(lane == 2 * r + term, value, coef_table)
    ints_ref[...] = int_table
    coefs_ref[...] = coef_table
    to_smem = [
        pltpu.make_async_copy(ints_ref, ints, table_sem.at[0]),
        pltpu.make_async_copy(coefs_ref, coefs, table_sem.at[1]),
    ]
    for copy in to_smem:
        copy.start()

    row = lax.broadcasted_iota(jnp.int32, (chan_count, LANES), 0)
    own = jnp.sum(jnp.where(row == me, source, 0), axis=0, keepdims=True)
    across = jnp.broadcast_to(own, (LANES, LANES))
    earlier = (across.T == across) & (at < to)
    arrival = own * bucket + jnp.sum(earlier.astype(jnp.int32), axis=0, keepdims=True)
    arrival_ref[...] = jnp.broadcast_to(arrival, arrival_ref.shape)

    for copy in to_smem:
        copy.wait()
    width = held.shape[2] // chunks
    tile_row = lax.broadcasted_iota(jnp.int32, (TILE, LANES), 0)
    for i in range(chunks):
        incoming[i].wait()
        columns = pl.ds(i * width, width)

        def to_one(d, carry):
            for r in range(bucket):
                entry = ints[d, r]
                slot = entry >> 2 * BITS
                c = sum((slot >= k * tiles_dev).astype(jnp.int32) for k in range(1, chans_dev))
                first_row = (blk * tiles_dev + slot - c * tiles_dev) * TILE
                live = live_ref[d * chans_dev + c] - first_row
                first = held[entry & LOW, :, columns].astype(jnp.float32)
                second = held[(entry >> BITS) & LOW, :, columns].astype(jnp.float32)
                keep = tile_row < live
                scale = [
                    jnp.tile(jnp.where(keep, coefs[d, 2 * r + term], 0.0), (1, width // LANES))
                    for term in range(2)
                ]
                value = scale[0] * first + scale[1] * second
                made[d * bucket + r, :, columns] = value.astype(jnp.bfloat16)
            return carry

        lax.fori_loop(0, chan_count, to_one, 0, unroll=2)
        outgoing[i].start()
    for copy in outgoing:
        copy.wait()


def recouple(live_rows, src_map, sixj, tiles, chan_count, chans_dev, chunks=3):
    slots = tiles.shape[0]
    sizes = (chan_count, chans_dev, slots // chans_dev, src_map.shape[2], chunks)
    table = jax.ShapeDtypeStruct((chan_count, LANES), jnp.int32)
    return pl.pallas_call(
        functools.partial(recouple_kernel, sizes),
        grid_spec=pltpu.PrefetchScalarGridSpec(
            num_scalar_prefetch=0,
            in_specs=[hbm_spec()] * 4,
            out_specs=[hbm_spec()] + [pl.BlockSpec(memory_space=pltpu.VMEM)] * 3,
            scratch_shapes=[
                pltpu.VMEM(tiles.shape, tiles.dtype),
                pltpu.VMEM(tiles.shape, tiles.dtype),
                pltpu.SMEM(live_rows.shape, jnp.int32),
                pltpu.VMEM(src_map.shape, jnp.int32),
                pltpu.VMEM(sixj.shape, jnp.float32),
                pltpu.VMEM((2, chans_dev, src_map.shape[1], LANES), jnp.int32),
                pltpu.VMEM((2, chans_dev, src_map.shape[1], LANES), jnp.float32),
                pltpu.SMEM(table.shape, jnp.int32),
                pltpu.SMEM(table.shape, jnp.float32),
                pltpu.SemaphoreType.DMA((chunks,)),
                pltpu.SemaphoreType.DMA((chunks,)),
                pltpu.SemaphoreType.DMA((5,)),
            ],
        ),
        out_shape=[
            jax.ShapeDtypeStruct(tiles.shape, tiles.dtype),
            table,
            jax.ShapeDtypeStruct(table.shape, jnp.float32),
            jax.ShapeDtypeStruct((TILE, LANES), jnp.int32),
        ],
        compiler_params=params(63),
    )(live_rows, src_map, sixj, tiles)


def product_kernel(
    start, block, arrival_hbm, x_ref, w_ref, out_ref,
    arrival_ref, rows, w_held, made, x_sem, w_sem, out_sem, table_sem,
):
    chans_dev, _, columns = w_ref.shape
    slots = x_ref.shape[0]
    part = slots // chans_dev
    steps = out_ref.shape[2] // block
    depth = w_held.shape[0]

    def x_copy(j, c):
        return pltpu.make_async_copy(x_ref.at[arrival_ref[0, j]], rows.at[j], x_sem.at[c])

    def w_copy(n, c):
        slot = lax.rem(n * chans_dev + c, depth)
        at = pl.ds(pl.multiple_of(start + n * block, block), block)
        return pltpu.make_async_copy(w_ref.at[c, :, at], w_held.at[slot], w_sem.at[slot])

    def out_copy(n):
        at = pl.ds(pl.multiple_of(n * block, block), block)
        return pltpu.make_async_copy(made.at[:, :, at], out_ref.at[:, :, at], out_sem.at[n])

    def x_all(c):
        tiles = pl.ds(c * part, part)
        return pltpu.make_async_copy(x_ref.at[tiles], rows.at[tiles], x_sem.at[c])

    def start_x(c):
        def one(j, carry):
            x_copy(j, c).start()
            return carry

        lax.fori_loop(c * part, (c + 1) * part, one, 0, unroll=8)

    table = pltpu.make_async_copy(arrival_hbm, arrival_ref, table_sem)
    table.start()
    w_copy(0, 0).start()
    table.wait()
    for c in range(chans_dev):
        if c:
            w_copy(0, c).start()
        start_x(c)

    def step(n, first):
        at = pl.ds(pl.multiple_of(n * block, block), block)
        for c in range(chans_dev):
            if first:
                x_all(c).wait()
            w_copy(n, c).wait()
            later = n * chans_dev + c + 2

            @pl.when(later < steps * chans_dev)
            def _():
                w_copy(later // chans_dev, later % chans_dev).start()

            left = rows[pl.ds(c * part, part)].reshape(part * TILE, columns)
            slot = lax.rem(n * chans_dev + c, depth)
            result = jnp.dot(left, w_held[slot], preferred_element_type=jnp.float32)
            result = result.astype(jnp.bfloat16).reshape(part, TILE, block)
            for i in range(part):
                made[arrival_ref[0, c * part + i], :, at] = result[i]

        out_copy(n).start()

    step(jnp.int32(0), True)

    def body(n, carry):
        step(n, False)
        return carry

    lax.fori_loop(1, steps, body, 0)
    for n in range(steps):
        out_copy(n).wait()


def product(arrival, x, w, start, width, block=512, depth=12):
    chans_dev, columns, _ = w.shape
    depth = min(depth, chans_dev * (width // block))
    made = jax.ShapeDtypeStruct(x.shape[:2] + (width,), x.dtype)
    return pl.pallas_call(
        functools.partial(product_kernel, start, block),
        grid_spec=pltpu.PrefetchScalarGridSpec(
            num_scalar_prefetch=0,
            in_specs=[hbm_spec()] * 3,
            out_specs=hbm_spec(),
            scratch_shapes=[
                pltpu.SMEM(arrival.shape, jnp.int32),
                pltpu.VMEM(x.shape, x.dtype),
                pltpu.VMEM((depth, columns, block), w.dtype),
                pltpu.VMEM(made.shape, x.dtype),
                pltpu.SemaphoreType.DMA((chans_dev,)),
                pltpu.SemaphoreType.DMA((depth,)),
                pltpu.SemaphoreType.DMA((width // block,)),
                pltpu.SemaphoreType.DMA,
            ],
        ),
        out_shape=made,
        compiler_params=params(63),
        cost_estimate=pl.CostEstimate(
            flops=2 * x.size * width,
            bytes_accessed=2 * (x.size + made.size + chans_dev * columns * width),
            transcendentals=0,
        ),
    )(arrival, x, w)


def finish_kernel(start, chunks, adds, writes, ints_hbm, coefs_hbm, back_ref, pair_ref, *refs):
    refs = list(refs)
    if start and writes:
        refs.pop(0)
    before_hbm = refs.pop(0) if start and adds else None
    out_ref = refs.pop(0) if writes else None
    energy_ref = refs.pop(0) if adds else None
    ints_ref, coefs_ref, before_ref, back, pair, made, slot_of, weight_of, back_sem, pair_sem, out_sem, table_sem = refs
    slots, _, columns = back.shape
    bucket = slots // ints_ref.shape[0]
    here = pl.ds(start, columns)
    incoming = [column_copies(back_ref, back, back_sem, chunks)]
    if adds:
        incoming.append(column_copies(pair_ref.at[:, :, here], pair, pair_sem, chunks))
    outgoing = column_copies(made, out_ref.at[:, :, here], out_sem, chunks) if writes else []
    tables = [
        pltpu.make_async_copy(ints_hbm, ints_ref, table_sem.at[0]),
        pltpu.make_async_copy(coefs_hbm, coefs_ref, table_sem.at[1]),
    ]
    if start and adds:
        earlier = pltpu.make_async_copy(before_hbm, before_ref, table_sem.at[2])
        tables.append(earlier)
    for copies in [tables] + list(zip(*incoming)):
        for copy in copies:
            copy.start()
    for copy in tables:
        copy.wait()

    def invert(d, carry):
        for r in range(bucket):
            entry = ints_ref[d, r]
            for term in range(2):
                g = (entry >> (term * BITS)) & LOW
                slot_of[term, g] = d * bucket + r
                weight_of[term, g] = coefs_ref[d, 2 * r + term]
        return carry

    lax.fori_loop(0, slots // bucket, invert, 0)
    width = columns // chunks
    total = jnp.zeros((TILE, width), jnp.float32)
    for i in range(chunks):
        for copies in incoming:
            copies[i].wait()
        at = pl.ds(i * width, width)

        def one(g, total):
            value = weight_of[0, g] * back[slot_of[0, g], :, at].astype(jnp.float32)
            value = value + weight_of[1, g] * back[slot_of[1, g], :, at].astype(jnp.float32)
            value = value.astype(jnp.bfloat16)
            if writes:
                made[g, :, at] = value
            if adds:
                total = total + value.astype(jnp.float32) * pair[g, :, at].astype(jnp.float32)
            return total

        total = lax.fori_loop(0, slots, one, total, unroll=8)
        if writes:
            outgoing[i].start()
    if adds:
        total = jnp.sum(jnp.sum(total, axis=0, keepdims=True), axis=1, keepdims=True)
        total = jnp.broadcast_to(total, energy_ref.shape)
        energy_ref[...] = total + before_ref[0:1, :] if start else total
    for copy in outgoing:
        copy.wait()


def finish(ints, coefs, back, pair, start, written, added, copies, chunks, adds=True, writes=True):
    energy = pl.BlockSpec(memory_space=pltpu.VMEM)
    again, more = bool(start and writes), bool(start and adds)
    outs = [(hbm_spec(), jax.ShapeDtypeStruct(pair.shape, pair.dtype))] * writes
    outs = outs + [(energy, jax.ShapeDtypeStruct((copies, LANES), jnp.float32))] * adds
    return pl.pallas_call(
        functools.partial(finish_kernel, start, chunks, adds, writes),
        grid_spec=pltpu.PrefetchScalarGridSpec(
            num_scalar_prefetch=0,
            in_specs=[hbm_spec()] * (4 + again + more),
            out_specs=[spec for spec, _ in outs],
            scratch_shapes=[
                pltpu.SMEM(ints.shape, jnp.int32),
                pltpu.SMEM(coefs.shape, jnp.float32),
                pltpu.VMEM((TILE, LANES), jnp.float32),
                pltpu.VMEM(back.shape, back.dtype),
                pltpu.VMEM(back.shape, back.dtype),
                pltpu.VMEM(back.shape, back.dtype),
                pltpu.SMEM((2, back.shape[0]), jnp.int32),
                pltpu.SMEM((2, back.shape[0]), jnp.float32),
                pltpu.SemaphoreType.DMA((chunks,)),
                pltpu.SemaphoreType.DMA((chunks,)),
                pltpu.SemaphoreType.DMA((chunks,)),
                pltpu.SemaphoreType.DMA((3,)),
            ],
        ),
        out_shape=[shape for _, shape in outs],
        input_output_aliases={4: 0} if again else {},
        compiler_params=params(63),
        cost_estimate=pl.CostEstimate(
            flops=6 * back.size, bytes_accessed=6 * back.size, transcendentals=0
        ),
    )(ints, coefs, back, pair, *[written] * again, *[added] * more)


def exchange(tiles, chan_count):
    parts = tiles.reshape((chan_count, -1) + tiles.shape[1:])
    return lax.all_to_all(parts, "chan", 0, 0, tiled=True).reshape(tiles.shape)


def on_device(pp_amps, ph_coupling, pp_coupling, sixj, src_map, live_rows):
    chan_count = lax.axis_size("chan")
    blk_count = lax.axis_size("blk")
    chans_dev, rows_dev, columns = pp_amps.shape
    slots = chans_dev * rows_dev // TILE
    own_tiles = pp_amps.reshape(slots, TILE, columns)
    pair_tiles = pp_coupling.reshape(slots, TILE, columns)
    sent, ints, coefs, arrival = recouple(
        live_rows, src_map, sixj, own_tiles, chan_count, chans_dev
    )
    got = exchange(sent, chan_count)
    cycle_pp = partial = None
    start = 0
    for width in WIDTHS:
        made = product(arrival, got, ph_coupling, start, width)
        back = exchange(made, chan_count)
        chunks = max(1, 4 * width // columns)
        last = start + width == columns
        copies = chan_count * blk_count if last else TILE
        call = functools.partial(
            finish, ints, coefs, back, pair_tiles, start, cycle_pp, partial, copies, chunks
        )
        start += width
        if last:
            (partial,) = call(writes=False)
            (cycle_pp,) = call(adds=False)
        else:
            cycle_pp, partial = call()
    parts = lax.all_to_all(partial, ("chan", "blk"), 0, 0, tiled=True)
    energy = jnp.sum(parts[:, 0]) / (columns * math.sqrt(chan_count * chans_dev))
    return (cycle_pp.reshape(pp_amps.shape), energy)


def solution(mesh):
    in_specs = (
        P("chan", "blk", None),
        P("chan", None, None),
        P("chan", "blk", None),
        P(),
        P(),
        P(),
    )
    out_specs = (P("chan", "blk", None), P())
    return jax.shard_map(
        on_device, mesh=mesh, in_specs=in_specs, out_specs=out_specs, check_vma=False
    )
```

```python
import functools
import math

import jax
import jax.numpy as jnp
from jax import lax
from jax.experimental import pallas as pl
from jax.experimental.pallas import tpu as pltpu
from jax.sharding import PartitionSpec as P

TILE = 8
LANES = 128
BITS = 8
LOW = (1 << BITS) - 1
WIDTHS = (1024, 2048)


def params(mib):
    return pltpu.CompilerParams(vmem_limit_bytes=mib * 1024 * 1024)


def hbm_spec():
    return pl.BlockSpec(memory_space=pltpu.HBM)


def column_copies(source, target, sems, count):
    width = source.shape[2] // count
    return [
        pltpu.make_async_copy(
            source.at[:, :, pl.ds(i * width, width)], target.at[:, :, pl.ds(i * width, width)], sems.at[i]
        )
        for i in range(count)
    ]


def floor_div(values, number):
    return jnp.floor((values.astype(jnp.float32) + 0.5) * (1.0 / number)).astype(jnp.int32)


def recouple_kernel(
    sizes, live_hbm, map_hbm, sixj_hbm, tiles_ref, send_ref, ints_ref, coefs_ref, arrival_ref,
    held, made, live_ref, map_ref, sixj_ref, map_buffer, sixj_buffer, ints, coefs, in_sem, out_sem, table_sem,
):
    chan_count, chans_dev, tiles_dev, all_tiles, chunks = sizes
    slots = chans_dev * tiles_dev
    bucket = slots // chan_count
    incoming = column_copies(tiles_ref, held, in_sem, chunks)
    outgoing = column_copies(made, send_ref, out_sem, chunks)
    from_hbm = [
        pltpu.make_async_copy(map_hbm, map_ref, table_sem.at[2]),
        pltpu.make_async_copy(sixj_hbm, sixj_ref, table_sem.at[3]),
        pltpu.make_async_copy(live_hbm, live_ref, table_sem.at[4]),
    ]
    for copy in from_hbm + incoming[:1]:
        copy.start()

    me = lax.axis_index("chan")
    blk = lax.axis_index("blk")
    lane = lax.broadcasted_iota(jnp.int32, (chan_count, LANES), 1)

    def slab(ref, buffer, term):
        whole = None
        for c in range(chans_dev):
            shift = lax.rem((c - blk) * tiles_dev + all_tiles, all_tiles)
            buffer[term, c] = pltpu.roll(ref[term], shift, axis=1)[:, :LANES]
            rows = buffer[term, c, pl.ds(c, chan_count, stride=chans_dev), :]
            whole = rows if c == 0 else jnp.where(lane < c * tiles_dev, whole, rows)
        return whole

    for copy in from_hbm:
        copy.wait()
    for copy in incoming[1:]:
        copy.start()
    source = None
    local = []
    for term in range(2):
        entry = slab(map_ref, map_buffer, term)
        channel = floor_div(entry, all_tiles)
        owner = floor_div(channel, chans_dev)
        tile = entry - channel * all_tiles - blk * tiles_dev
        local.append((channel - owner * chans_dev) * tiles_dev + tile)
        source = owner if source is None else source
    weight = [slab(sixj_ref, sixj_buffer, term) for term in range(2)]

    mine = (lane < slots) & (source == me)
    at = lax.broadcasted_iota(jnp.int32, (LANES, LANES), 0)
    to = lax.broadcasted_iota(jnp.int32, (LANES, LANES), 1)
    upto = (at <= to).astype(jnp.bfloat16)
    rank = jnp.dot(mine.astype(jnp.bfloat16), upto, preferred_element_type=jnp.float32)
    rank = rank.astype(jnp.int32) - 1
    packed = local[0] + (local[1] << BITS) + (lane << 2 * BITS)
    int_table = jnp.zeros((chan_count, LANES), jnp.int32)
    coef_table = jnp.zeros((chan_count, LANES), jnp.float32)
    for r in range(bucket):
        chosen = mine & (rank == r)
        value = jnp.sum(jnp.where(chosen, packed, 0), axis=1, keepdims=True)
        int_table = jnp.where(lane == r, value, int_table)
        for term, values in enumerate(weight):
            value = jnp.sum(jnp.where(chosen, values, 0.0), axis=1, keepdims=True)
            coef_table = jnp.where(lane == 2 * r + term, value, coef_table)
    ints_ref[...] = int_table
    coefs_ref[...] = coef_table
    to_smem = [
        pltpu.make_async_copy(ints_ref, ints, table_sem.at[0]),
        pltpu.make_async_copy(coefs_ref, coefs, table_sem.at[1]),
    ]
    for copy in to_smem:
        copy.start()

    row = lax.broadcasted_iota(jnp.int32, (chan_count, LANES), 0)
    own = jnp.sum(jnp.where(row == me, source, 0), axis=0, keepdims=True)
    across = jnp.broadcast_to(own, (LANES, LANES))
    earlier = (across.T == across) & (at < to)
    arrival = own * bucket + jnp.sum(earlier.astype(jnp.int32), axis=0, keepdims=True)
    arrival_ref[...] = jnp.broadcast_to(arrival, arrival_ref.shape)

    for copy in to_smem:
        copy.wait()
    width = held.shape[2] // chunks
    tile_row = lax.broadcasted_iota(jnp.int32, (TILE, LANES), 0)
    for i in range(chunks):
        incoming[i].wait()
        columns = pl.ds(i * width, width)

        def to_one(d, carry):
            for r in range(bucket):
                entry = ints[d, r]
                slot = entry >> 2 * BITS
                c = sum((slot >= k * tiles_dev).astype(jnp.int32) for k in range(1, chans_dev))
                first_row = (blk * tiles_dev + slot - c * tiles_dev) * TILE
                live = live_ref[d * chans_dev + c] - first_row
                first = held[entry & LOW, :, columns].astype(jnp.float32)
                second = held[(entry >> BITS) & LOW, :, columns].astype(jnp.float32)
                keep = tile_row < live
                scale = [
                    jnp.tile(jnp.where(keep, coefs[d, 2 * r + term], 0.0), (1, width // LANES))
                    for term in range(2)
                ]
                value = scale[0] * first + scale[1] * second
                made[d * bucket + r, :, columns] = value.astype(jnp.bfloat16)
            return carry

        lax.fori_loop(0, chan_count, to_one, 0, unroll=2)
        outgoing[i].start()
    for copy in outgoing:
        copy.wait()


def recouple(live_rows, src_map, sixj, tiles, chan_count, chans_dev, chunks=3):
    slots = tiles.shape[0]
    sizes = (chan_count, chans_dev, slots // chans_dev, src_map.shape[2], chunks)
    table = jax.ShapeDtypeStruct((chan_count, LANES), jnp.int32)
    return pl.pallas_call(
        functools.partial(recouple_kernel, sizes),
        grid_spec=pltpu.PrefetchScalarGridSpec(
            num_scalar_prefetch=0,
            in_specs=[hbm_spec()] * 4,
            out_specs=[hbm_spec()] + [pl.BlockSpec(memory_space=pltpu.VMEM)] * 3,
            scratch_shapes=[
                pltpu.VMEM(tiles.shape, tiles.dtype),
                pltpu.VMEM(tiles.shape, tiles.dtype),
                pltpu.SMEM(live_rows.shape, jnp.int32),
                pltpu.VMEM(src_map.shape, jnp.int32),
                pltpu.VMEM(sixj.shape, jnp.float32),
                pltpu.VMEM((2, chans_dev, src_map.shape[1], LANES), jnp.int32),
                pltpu.VMEM((2, chans_dev, src_map.shape[1], LANES), jnp.float32),
                pltpu.SMEM(table.shape, jnp.int32),
                pltpu.SMEM(table.shape, jnp.float32),
                pltpu.SemaphoreType.DMA((chunks,)),
                pltpu.SemaphoreType.DMA((chunks,)),
                pltpu.SemaphoreType.DMA((5,)),
            ],
        ),
        out_shape=[
            jax.ShapeDtypeStruct(tiles.shape, tiles.dtype),
            table,
            jax.ShapeDtypeStruct(table.shape, jnp.float32),
            jax.ShapeDtypeStruct((TILE, LANES), jnp.int32),
        ],
        compiler_params=params(63),
    )(live_rows, src_map, sixj, tiles)


def product_kernel(
    start, block, arrival_hbm, x_ref, w_ref, out_ref,
    arrival_ref, rows, w_held, made, x_sem, w_sem, out_sem, table_sem,
):
    chans_dev, _, columns = w_ref.shape
    slots = x_ref.shape[0]
    part = slots // chans_dev
    steps = out_ref.shape[2] // block
    depth = w_held.shape[0]

    def x_copy(j, c):
        return pltpu.make_async_copy(x_ref.at[arrival_ref[0, j]], rows.at[j], x_sem.at[c])

    def w_copy(n, c):
        slot = lax.rem(n * chans_dev + c, depth)
        at = pl.ds(pl.multiple_of(start + n * block, block), block)
        return pltpu.make_async_copy(w_ref.at[c, :, at], w_held.at[slot], w_sem.at[slot])

    def out_copy(n):
        at = pl.ds(pl.multiple_of(n * block, block), block)
        return pltpu.make_async_copy(made.at[:, :, at], out_ref.at[:, :, at], out_sem.at[n])

    def x_all(c):
        tiles = pl.ds(c * part, part)
        return pltpu.make_async_copy(x_ref.at[tiles], rows.at[tiles], x_sem.at[c])

    def start_x(c):
        def one(j, carry):
            x_copy(j, c).start()
            return carry

        lax.fori_loop(c * part, (c + 1) * part, one, 0, unroll=8)

    table = pltpu.make_async_copy(arrival_hbm, arrival_ref, table_sem)
    table.start()
    w_copy(0, 0).start()
    table.wait()
    for c in range(chans_dev):
        if c:
            w_copy(0, c).start()
        start_x(c)

    def step(n, first):
        at = pl.ds(pl.multiple_of(n * block, block), block)
        for c in range(chans_dev):
            if first:
                x_all(c).wait()
            w_copy(n, c).wait()
            later = n * chans_dev + c + 2

            @pl.when(later < steps * chans_dev)
            def _():
                w_copy(later // chans_dev, later % chans_dev).start()

            left = rows[pl.ds(c * part, part)].reshape(part * TILE, columns)
            slot = lax.rem(n * chans_dev + c, depth)
            result = jnp.dot(left, w_held[slot], preferred_element_type=jnp.float32)
            result = result.astype(jnp.bfloat16).reshape(part, TILE, block)
            for i in range(part):
                made[arrival_ref[0, c * part + i], :, at] = result[i]

        out_copy(n).start()

    step(jnp.int32(0), True)

    def body(n, carry):
        step(n, False)
        return carry

    lax.fori_loop(1, steps, body, 0)
    for n in range(steps):
        out_copy(n).wait()


def product(arrival, x, w, start, width, block=512, depth=12):
    chans_dev, columns, _ = w.shape
    depth = min(depth, chans_dev * (width // block))
    made = jax.ShapeDtypeStruct(x.shape[:2] + (width,), x.dtype)
    return pl.pallas_call(
        functools.partial(product_kernel, start, block),
        grid_spec=pltpu.PrefetchScalarGridSpec(
            num_scalar_prefetch=0,
            in_specs=[hbm_spec()] * 3,
            out_specs=hbm_spec(),
            scratch_shapes=[
                pltpu.SMEM(arrival.shape, jnp.int32),
                pltpu.VMEM(x.shape, x.dtype),
                pltpu.VMEM((depth, columns, block), w.dtype),
                pltpu.VMEM(made.shape, x.dtype),
                pltpu.SemaphoreType.DMA((chans_dev,)),
                pltpu.SemaphoreType.DMA((depth,)),
                pltpu.SemaphoreType.DMA((width // block,)),
                pltpu.SemaphoreType.DMA,
            ],
        ),
        out_shape=made,
        compiler_params=params(63),
        cost_estimate=pl.CostEstimate(
            flops=2 * x.size * width,
            bytes_accessed=2 * (x.size + made.size + chans_dev * columns * width),
            transcendentals=0,
        ),
    )(arrival, x, w)


def finish_kernel(start, chunks, adds, writes, ints_hbm, coefs_hbm, back_ref, pair_ref, *refs):
    refs = list(refs)
    if start and writes:
        refs.pop(0)
    before_hbm = refs.pop(0) if start and adds else None
    out_ref = refs.pop(0) if writes else None
    energy_ref = refs.pop(0) if adds else None
    ints_ref, coefs_ref, before_ref, back, pair, made, slot_of, weight_of, back_sem, pair_sem, out_sem, table_sem = refs
    slots, _, columns = back.shape
    bucket = slots // ints_ref.shape[0]
    here = pl.ds(start, columns)
    incoming = [column_copies(back_ref, back, back_sem, chunks)]
    if adds:
        incoming.append(column_copies(pair_ref.at[:, :, here], pair, pair_sem, chunks))
    outgoing = column_copies(made, out_ref.at[:, :, here], out_sem, chunks) if writes else []
    tables = [
        pltpu.make_async_copy(ints_hbm, ints_ref, table_sem.at[0]),
        pltpu.make_async_copy(coefs_hbm, coefs_ref, table_sem.at[1]),
    ]
    if start and adds:
        earlier = pltpu.make_async_copy(before_hbm, before_ref, table_sem.at[2])
        tables.append(earlier)
    for copies in [tables] + list(zip(*incoming)):
        for copy in copies:
            copy.start()
    for copy in tables:
        copy.wait()

    def invert(d, carry):
        for r in range(bucket):
            entry = ints_ref[d, r]
            for term in range(2):
                g = (entry >> (term * BITS)) & LOW
                slot_of[term, g] = d * bucket + r
                weight_of[term, g] = coefs_ref[d, 2 * r + term]
        return carry

    lax.fori_loop(0, slots // bucket, invert, 0)
    width = columns // chunks
    total = jnp.zeros((TILE, width), jnp.float32)
    for i in range(chunks):
        for copies in incoming:
            copies[i].wait()
        at = pl.ds(i * width, width)

        def one(g, total):
            value = weight_of[0, g] * back[slot_of[0, g], :, at].astype(jnp.float32)
            value = value + weight_of[1, g] * back[slot_of[1, g], :, at].astype(jnp.float32)
            value = value.astype(jnp.bfloat16)
            if writes:
                made[g, :, at] = value
            if adds:
                total = total + value.astype(jnp.float32) * pair[g, :, at].astype(jnp.float32)
            return total

        total = lax.fori_loop(0, slots, one, total, unroll=8)
        if writes:
            outgoing[i].start()
    if adds:
        total = jnp.sum(jnp.sum(total, axis=0, keepdims=True), axis=1, keepdims=True)
        total = jnp.broadcast_to(total, energy_ref.shape)
        energy_ref[...] = total + before_ref[0:1, :] if start else total
    for copy in outgoing:
        copy.wait()


def finish(ints, coefs, back, pair, start, written, added, copies, chunks, adds=True, writes=True):
    energy = pl.BlockSpec(memory_space=pltpu.VMEM)
    again, more = bool(start and writes), bool(start and adds)
    outs = [(hbm_spec(), jax.ShapeDtypeStruct(pair.shape, pair.dtype))] * writes
    outs = outs + [(energy, jax.ShapeDtypeStruct((copies, LANES), jnp.float32))] * adds
    return pl.pallas_call(
        functools.partial(finish_kernel, start, chunks, adds, writes),
        grid_spec=pltpu.PrefetchScalarGridSpec(
            num_scalar_prefetch=0,
            in_specs=[hbm_spec()] * (4 + again + more),
            out_specs=[spec for spec, _ in outs],
            scratch_shapes=[
                pltpu.SMEM(ints.shape, jnp.int32),
                pltpu.SMEM(coefs.shape, jnp.float32),
                pltpu.VMEM((TILE, LANES), jnp.float32),
                pltpu.VMEM(back.shape, back.dtype),
                pltpu.VMEM(back.shape, back.dtype),
                pltpu.VMEM(back.shape, back.dtype),
                pltpu.SMEM((2, back.shape[0]), jnp.int32),
                pltpu.SMEM((2, back.shape[0]), jnp.float32),
                pltpu.SemaphoreType.DMA((chunks,)),
                pltpu.SemaphoreType.DMA((chunks,)),
                pltpu.SemaphoreType.DMA((chunks,)),
                pltpu.SemaphoreType.DMA((3,)),
            ],
        ),
        out_shape=[shape for _, shape in outs],
        input_output_aliases={4: 0} if again else {},
        compiler_params=params(63),
        cost_estimate=pl.CostEstimate(
            flops=6 * back.size, bytes_accessed=6 * back.size, transcendentals=0
        ),
    )(ints, coefs, back, pair, *[written] * again, *[added] * more)


def exchange(tiles, chan_count):
    parts = tiles.reshape((chan_count, -1) + tiles.shape[1:])
    return lax.all_to_all(parts, "chan", 0, 0, tiled=True).reshape(tiles.shape)


def on_device(pp_amps, ph_coupling, pp_coupling, sixj, src_map, live_rows):
    chan_count = lax.axis_size("chan")
    blk_count = lax.axis_size("blk")
    chans_dev, rows_dev, columns = pp_amps.shape
    slots = chans_dev * rows_dev // TILE
    own_tiles = pp_amps.reshape(slots, TILE, columns)
    pair_tiles = pp_coupling.reshape(slots, TILE, columns)
    sent, ints, coefs, arrival = recouple(
        live_rows, src_map, sixj, own_tiles, chan_count, chans_dev
    )
    got = exchange(sent, chan_count)
    cycle_pp = partial = None
    start = 0
    for width in WIDTHS:
        made = product(arrival, got, ph_coupling, start, width)
        back = exchange(made, chan_count)
        chunks = max(1, 4 * width // columns)
        last = start + width == columns
        copies = chan_count * blk_count if last else TILE
        call = functools.partial(
            finish, ints, coefs, back, pair_tiles, start, cycle_pp, partial, copies, chunks
        )
        start += width
        cycle_pp, partial = call()
    parts = lax.all_to_all(partial, ("chan", "blk"), 0, 0, tiled=True)
    energy = jnp.sum(parts[:, 0]) / (columns * math.sqrt(chan_count * chans_dev))
    return (cycle_pp.reshape(pp_amps.shape), energy)


def solution(mesh):
    in_specs = (
        P("chan", "blk", None),
        P("chan", None, None),
        P("chan", "blk", None),
        P(),
        P(),
        P(),
    )
    out_specs = (P("chan", "blk", None), P())
    return jax.shard_map(
        on_device, mesh=mesh, in_specs=in_specs, out_specs=out_specs, check_vma=False
    )
```
